32 devices in a mesh: dp: 16 (over z, y, core), tensor: 2 (over x).
Axes of the slice: x: 2, y: 2, z: 4, core: 2. Of those that a mesh axis runs over, the one named last changes fastest.
Arguments:
- tokens: int32 [32, 1024], P('dp'), may hold values from 0 to 255
- targets: int32 [32, 1024], P('dp'), may hold values from 0 to 255
- boundaries: int32 [32, 1024], P('dp'), may hold values from 0 to 1, as said below
- lengths: int32 [32], P('dp'), may hold values from 128 to 1024
- embedding: float32 [256, 512], replicated, may hold values from -6 to 6
- head: float32 [512, 256], replicated, may hold values from -0.25 to 0.25
- qkv_weight: float32 [3, 512, 3, 512], P(None, None, None, 'tensor'), may hold values from -0.25 to 0.25
- out_weight: float32 [3, 512, 512], P(None, 'tensor')
- up_weight: float32 [3, 512, 2048], P(None, None, 'tensor'), may hold values from -0.25 to 0.25
- up_bias: float32 [3, 2048], P(None, 'tensor'), may hold values from -1.8 to 1.8
- down_weight: float32 [3, 2048, 512], P(None, 'tensor')
- gains: float32 [7, 512], replicated, may hold values from 0.5 to 1.5
- boundary_weight: float32 [512], replicated, may hold values from -0.25 to 0.25
- qkv_moment: float32 [3, 512, 3, 512], P(None, None, None, 'tensor')
- out_moment: float32 [3, 512, 512], P(None, 'tensor')
- up_moment: float32 [3, 512, 2048], P(None, None, 'tensor')
- down_moment: float32 [3, 2048, 512], P(None, 'tensor')
- embedding_first: float32 [256, 512], replicated
- embedding_second: float32 [256, 512], replicated
- head_first: float32 [512, 256], replicated
- head_second: float32 [512, 256], replicated
- gains_first: float32 [7, 512], replicated
- gains_second: float32 [7, 512], replicated
- bias_first: float32 [3, 2048], P(None, 'tensor')
- bias_second: float32 [3, 2048], P(None, 'tensor')
- boundary_first: float32 [512], replicated
- boundary_second: float32 [512], replicated
Outputs:
- loss_sum: float32 [], replicated
- token_count: float32 [], replicated
- grad_norm: float32 [], replicated
- qkv_moment_new: float32 [3, 512, 3, 512], P(None, None, None, 'tensor')
- qkv_new: float32 [3, 512, 3, 512], P(None, None, None, 'tensor')
- out_moment_new: float32 [3, 512, 512], P(None, 'tensor')
- out_new: float32 [3, 512, 512], P(None, 'tensor')
- up_moment_new: float32 [3, 512, 2048], P(None, None, 'tensor')
- up_new: float32 [3, 512, 2048], P(None, None, 'tensor')
- down_moment_new: float32 [3, 2048, 512], P(None, 'tensor')
- down_new: float32 [3, 2048, 512], P(None, 'tensor')
- embedding_first_new: float32 [256, 512], replicated
- embedding_second_new: float32 [256, 512], replicated
- embedding_new: float32 [256, 512], replicated
- head_first_new: float32 [512, 256], replicated
- head_second_new: float32 [512, 256], replicated
- head_new: float32 [512, 256], replicated
- gains_first_new: float32 [7, 512], replicated
- gains_second_new: float32 [7, 512], replicated
- gains_new: float32 [7, 512], replicated
- bias_first_new: float32 [3, 2048], P(None, 'tensor')
- bias_second_new: float32 [3, 2048], P(None, 'tensor')
- bias_new: float32 [3, 2048], P(None, 'tensor')
- boundary_first_new: float32 [512], replicated
- boundary_second_new: float32 [512], replicated
- boundary_new: float32 [512], replicated
The draws below stay inside these ranges and needn't reach their ends.
Inputs may be any that keep to these rules, and one draw needn't show every extreme that they name: `boundaries`: each sequence holds exactly 160 segments; the last byte of every sequence is a 1.
All inputs are finite; a program needn't handle non-finite values.
Results may differ from the reference program's by a relative error of at most 0.025.
Values may be sent and summed in bfloat16 or wider, within the bound.
No kernel may reach another device: no remote copies, remote signals or barrier semaphores. Data moves between devices by JAX's collectives and lax.ppermute only.
A program may use at most 448 MiB of HBM per device.

```python
import math
import jax
import jax.numpy as jnp
from jax import lax

D = 512
HEADS = 8
HEAD_SIZE = 64
FF = 2048
VOCAB = 256
LAYERS = 3
LEN = 1024
SHORT = 160
STEP = 10
SEQ_DEV = 2
SEQS = 32
PARAMS = 9709568
N_DP = 16
N_TENSOR = 2


def gradient_size(factor):
    return factor * 0.05 / math.sqrt(PARAMS)


def moment_one(key, shape, factor):
    return jax.random.normal(key, shape, jnp.float32) * (0.11 * gradient_size(factor))


def moment_two(key, shape, factor):
    spread = jnp.exp(jax.random.uniform(key, shape, jnp.float32, 0.0, math.log(4.0)))
    return spread * (0.05 / 0.95 * gradient_size(factor) ** 2)


def momentum_draw(key, shape):
    return jax.random.normal(key, shape, jnp.float32) * gradient_size(1.0)


def rising_rows(key, shape, scale, rise):
    ramp = 1.0 + rise * jnp.arange(shape[1], dtype=jnp.float32) / (shape[1] - 1)
    return jax.random.normal(key, shape, jnp.float32) * ramp[None, :, None] * scale


def one_sequence(key):
    key_lens, key_pick, key_split = jax.random.split(key, 3)
    short_ids = jnp.arange(SHORT, dtype=jnp.int32)
    seg_lens = jax.random.randint(key_lens, (SHORT,), 2, 7)
    picked = jax.random.permutation(key_pick, SHORT)[:2]
    is_long = (short_ids == picked[0]) | (short_ids == picked[1])
    remain = LEN - jnp.sum(jnp.where(is_long, 0, seg_lens))
    quarter = remain // 4
    first_long = remain // 2 + jax.random.randint(key_split, (), -quarter, quarter + 1)
    long_lens = jnp.where(short_ids == picked[0], first_long, remain - first_long)
    seg_lens = jnp.where(is_long, long_lens, seg_lens)
    ends = jnp.cumsum(seg_lens) - 1
    marks = jnp.any(jnp.arange(LEN, dtype=jnp.int32)[:, None] == ends[None, :], axis=1)
    return marks.astype(jnp.int32)


def draw_boundaries(key, part):
    key = jax.random.fold_in(key, 1)
    return jax.vmap(one_sequence)(jax.random.split(key, SEQS)).astype(jnp.int32)


def draw_lengths(key, part):
    key = jax.random.fold_in(key, 2)
    seq_total = SEQ_DEV * N_DP
    dp_place = jnp.arange(seq_total, dtype=jnp.int32) // SEQ_DEV
    base_length = LEN * (N_DP - 1 + 2 * dp_place) // (3 * (N_DP - 1))
    jitter = jax.random.randint(key, (seq_total,), 0, LEN // 8 + 1)
    last_one = jnp.arange(seq_total, dtype=jnp.int32) == seq_total - 1
    return jnp.where(last_one, LEN, base_length - jitter).astype(jnp.int32)


def draw_out_weight(key, part):
    key = jax.random.fold_in(key, 3)
    scale = math.sqrt(LEN / (32.0 * D))
    return rising_rows(key, (LAYERS, D, D), scale, 2.0)


def draw_down_weight(key, part):
    key = jax.random.fold_in(key, 4)
    scale = 1.0 / math.sqrt(FF)
    return rising_rows(key, (LAYERS, FF, D), scale, 2.0)


def draw_qkv_moment(key, part):
    return momentum_draw(jax.random.fold_in(key, 5), (LAYERS, D, 3, D))


def draw_out_moment(key, part):
    return momentum_draw(jax.random.fold_in(key, 6), (LAYERS, D, D))


def draw_up_moment(key, part):
    return momentum_draw(jax.random.fold_in(key, 7), (LAYERS, D, FF))


def draw_down_moment(key, part):
    return momentum_draw(jax.random.fold_in(key, 8), (LAYERS, FF, D))


def draw_embedding_first(key, part):
    return moment_one(jax.random.fold_in(key, 9), (VOCAB, D), 0.5)


def draw_embedding_second(key, part):
    return moment_two(jax.random.fold_in(key, 10), (VOCAB, D), 0.5)


def draw_head_first(key, part):
    return moment_one(jax.random.fold_in(key, 11), (D, VOCAB), 1.0)


def draw_head_second(key, part):
    return moment_two(jax.random.fold_in(key, 12), (D, VOCAB), 1.0)


def draw_gains_first(key, part):
    return moment_one(jax.random.fold_in(key, 13), (2 * LAYERS + 1, D), 5.0)


def draw_gains_second(key, part):
    return moment_two(jax.random.fold_in(key, 14), (2 * LAYERS + 1, D), 5.0)


def draw_bias_first(key, part):
    return moment_one(jax.random.fold_in(key, 15), (LAYERS, FF), 1.0)


def draw_bias_second(key, part):
    return moment_two(jax.random.fold_in(key, 16), (LAYERS, FF), 1.0)


def draw_boundary_first(key, part):
    return moment_one(jax.random.fold_in(key, 17), (D,), 2.0)


def draw_boundary_second(key, part):
    return moment_two(jax.random.fold_in(key, 18), (D,), 2.0)


def plant(array, own_key, low, largest):
    place = [jax.random.randint(jax.random.fold_in(own_key, axis), (), 0, length) for axis, length in enumerate(array.shape)]
    main_axis = array.shape.index(max(array.shape))
    neighbour = place[:main_axis] + [(place[main_axis] + 1) % array.shape[main_axis]] + place[main_axis + 1:]
    return array.at[tuple(place)].set(low).at[tuple(neighbour)].set(largest)


def shard_levels(rng, extent, shards, low, largest):
    loudness = 1.0
    for axis_at, shards_of in shards:
        steps = jax.random.uniform(jax.random.fold_in(jax.random.fold_in(rng, 6), axis_at), (shards_of,), jnp.float32, low / len(shards), largest / len(shards))
        loudness = loudness * jnp.repeat(jnp.exp(steps), extent[axis_at] // shards_of).reshape((-1,) + (1,) * (len(extent) - 1 - axis_at))
    return loudness


def centred(rng, shape, width, reach, cuts=(), held_as=jnp.bfloat16):
    gain = shard_levels(rng, shape, cuts, -0.22, 0.18) if cuts else 1.0
    result = jax.random.normal(rng, shape, jnp.float32) * width * gain
    return jnp.minimum(jnp.maximum(result, -reach), reach).astype(held_as)


def setup_inputs(seed: int = 0) -> dict:
    splits = jax.random.split(jax.random.key(seed), 28)
    tokens = plant(jax.random.randint(splits[0], (SEQS, LEN), 0, VOCAB), jax.random.fold_in(splits[0], 1), 0, VOCAB - 1).astype(jnp.int32)
    targets = plant(jax.random.randint(splits[1], (SEQS, LEN), 0, VOCAB), jax.random.fold_in(splits[1], 1), 0, VOCAB - 1).astype(jnp.int32)
    boundaries = draw_boundaries(jax.random.fold_in(splits[27], 71), 0)
    lengths = draw_lengths(jax.random.fold_in(splits[27], 71), 0)
    embedding = centred(splits[4], (VOCAB, D), 1.0, 6.0, (), jnp.float32)
    head = centred(splits[5], (D, VOCAB), D ** -0.5, 0.25, (), jnp.float32)
    qkv_weight = centred(splits[6], (LAYERS, D, 3, D), D ** -0.5, 0.25, ((3, 2),), jnp.float32)
    out_weight = draw_out_weight(jax.random.fold_in(splits[27], 71), 0)
    up_weight = centred(splits[8], (LAYERS, D, FF), D ** -0.5, 0.25, ((2, 2),), jnp.float32)
    up_bias = centred(splits[9], (LAYERS, FF), 0.3, 1.8, ((1, 2),), jnp.float32)
    down_weight = draw_down_weight(jax.random.fold_in(splits[27], 71), 0)
    gains = jnp.clip(1.0 + 0.1 * jax.random.normal(splits[11], (2 * LAYERS + 1, D), jnp.float32), 0.5, 1.5)
    boundary_weight = centred(splits[12], (D,), D ** -0.5, 0.25, (), jnp.float32)
    qkv_moment = draw_qkv_moment(jax.random.fold_in(splits[27], 71), 0)
    out_moment = draw_out_moment(jax.random.fold_in(splits[27], 71), 0)
    up_moment = draw_up_moment(jax.random.fold_in(splits[27], 71), 0)
    down_moment = draw_down_moment(jax.random.fold_in(splits[27], 71), 0)
    embedding_first = draw_embedding_first(jax.random.fold_in(splits[27], 71), 0)
    embedding_second = draw_embedding_second(jax.random.fold_in(splits[27], 71), 0)
    head_first = draw_head_first(jax.random.fold_in(splits[27], 71), 0)
    head_second = draw_head_second(jax.random.fold_in(splits[27], 71), 0)
    gains_first = draw_gains_first(jax.random.fold_in(splits[27], 71), 0)
    gains_second = draw_gains_second(jax.random.fold_in(splits[27], 71), 0)
    bias_first = draw_bias_first(jax.random.fold_in(splits[27], 71), 0)
    bias_second = draw_bias_second(jax.random.fold_in(splits[27], 71), 0)
    boundary_first = draw_boundary_first(jax.random.fold_in(splits[27], 71), 0)
    boundary_second = draw_boundary_second(jax.random.fold_in(splits[27], 71), 0)
    return dict(tokens=tokens, targets=targets, boundaries=boundaries, lengths=lengths, embedding=embedding, head=head, qkv_weight=qkv_weight, out_weight=out_weight, up_weight=up_weight, up_bias=up_bias, down_weight=down_weight, gains=gains, boundary_weight=boundary_weight, qkv_moment=qkv_moment, out_moment=out_moment, up_moment=up_moment, down_moment=down_moment, embedding_first=embedding_first, embedding_second=embedding_second, head_first=head_first, head_second=head_second, gains_first=gains_first, gains_second=gains_second, bias_first=bias_first, bias_second=bias_second, boundary_first=boundary_first, boundary_second=boundary_second)


NORM_EPSILON = 1e-06
PRIOR_RATE = 0.25
CLIP_NORM = 0.05
MOMENTUM = 0.95
MUON_DECAY = 0.01
MUON_RATE = 4.0
BETA_ONE = 0.9
BETA_TWO = 0.95
ADAM_EPSILON = 1e-08
COEF_A = 3.4445
COEF_B = -4.775
COEF_C = 2.0315

@jax.custom_vjp
def low(v):
    return lax.optimization_barrier(v.astype(jnp.bfloat16)).astype(jnp.float32)

@jax.custom_vjp
def low_back(v):
    return v

def low_keep(v):
    return (low(v), None)

def low_pass(kept, grad):
    return (grad,)

def back_keep(v):
    return (v, None)

def back_low(kept, grad):
    return (low(grad),)
low.defvjp(low_keep, low_pass)
low_back.defvjp(back_keep, back_low)

def matmul(left, right):
    return jnp.dot(left, right, precision=lax.Precision.HIGHEST)

def rms_norm(values, gain_row):
    return values * lax.rsqrt(lax.optimization_barrier(jnp.mean(values * values, axis=-1, keepdims=True)) + NORM_EPSILON) * gain_row

def group_sum(inputs, weight):
    parts = jnp.einsum('tgi,gio->gto', inputs.reshape(inputs.shape[0], N_TENSOR, -1), weight.reshape(N_TENSOR, -1, weight.shape[1]), precision=lax.Precision.HIGHEST)
    return low_back(lax.optimization_barrier(jnp.sum(low(parts), axis=0)))

def attention(normed, w_qkv, w_out):
    length = normed.shape[0]
    packed = low_back(low(jnp.einsum('td,dcf->tcf', normed, w_qkv, precision=lax.Precision.HIGHEST)))
    queries = packed[:, 0].reshape(length, HEADS, HEAD_SIZE)
    key_rows = packed[:, 1].reshape(length, HEADS, HEAD_SIZE)
    value_rows = packed[:, 2].reshape(length, HEADS, HEAD_SIZE)
    scores = low_back(jnp.einsum('qhd,khd->hqk', queries, key_rows, precision=lax.Precision.HIGHEST) * HEAD_SIZE ** (-0.5))
    allowed = jnp.arange(length)[:, None] >= jnp.arange(length)[None, :]
    scores = jnp.where(allowed[None], scores, -1e+30)
    highest = lax.optimization_barrier(jnp.max(scores, axis=-1, keepdims=True))
    expo = jnp.exp(scores - highest)
    softened = low(expo / lax.optimization_barrier(jnp.sum(expo, axis=-1, keepdims=True)))
    mixed = jnp.einsum('hqk,khd->qhd', softened, value_rows, precision=lax.Precision.HIGHEST)
    mixed = low_back(low(mixed)).reshape(length, D)
    return group_sum(mixed, w_out)

def layer(inputs, gain_pair, w_qkv, w_out, w_up, b_up, w_down):
    after = inputs + attention(low(rms_norm(inputs, gain_pair[0])), w_qkv, w_out)
    normed = low(rms_norm(after, gain_pair[1]))
    hidden = low_back(matmul(normed, w_up) + b_up)
    return after + group_sum(low(jax.nn.gelu(hidden)), w_down)

def forward(params, tokens, targets, boundaries, counted):
    embed, head, w_qkv, w_out, w_up, b_up, w_down, gains, w_bound = params
    w_qkv, w_out, w_up, w_down, head_low = (low(w_qkv), low(w_out), low(w_up), low(w_down), low(head))

    def layer_at(index, inputs):
        return layer(inputs, gains[2 * index:2 * index + 2], w_qkv[index], w_out[index], w_up[index], b_up[index], w_down[index])

    def first_section(item):
        token_row, mask_row = item
        hidden = layer_at(0, embed[token_row])
        probs = jax.nn.sigmoid(matmul(hidden, w_bound))
        return (hidden, jnp.sum(mask_row * probs))
    hidden_all, bound_sums = lax.map(jax.checkpoint(first_section), (tokens, counted))
    bound_total = jnp.sum(bound_sums)
    count_total = jnp.sum(counted)
    short_ids = jnp.arange(SHORT, dtype=jnp.int32)
    vocab_ids = jnp.arange(VOCAB, dtype=jnp.int32)

    def second_section(item):
        hidden, bound_row, target_row, mask_row = item
        segment = (jnp.cumsum(bound_row) - bound_row).astype(jnp.int32)
        pool_hot = (segment[None, :] == short_ids[:, None]).astype(jnp.float32)
        sizes_seg = lax.optimization_barrier(jnp.sum(pool_hot, axis=1, keepdims=True))
        shortened = low_back(matmul(pool_hot, low(hidden))) / sizes_seg
        short_out = layer_at(1, shortened)
        lift_hot = (segment[:, None] - 1 == short_ids[None, :]).astype(jnp.float32)
        merged = hidden + low_back(matmul(lift_hot, low(short_out)))
        final = layer_at(2, merged)
        logits = low_back(matmul(low(rms_norm(final, gains[2 * LAYERS])), head_low))
        highest = lax.optimization_barrier(jnp.max(logits, axis=-1, keepdims=True))
        log_probs = logits - highest - jnp.log(lax.optimization_barrier(jnp.sum(jnp.exp(logits - highest), axis=-1, keepdims=True)))
        picked = lax.optimization_barrier(jnp.sum(jnp.where(target_row[:, None] == vocab_ids[None, :], log_probs, 0.0), axis=-1))
        return -jnp.sum(mask_row * picked)
    losses = lax.map(jax.checkpoint(second_section), (hidden_all, boundaries, targets, counted))
    rest_count = count_total - bound_total
    prior_nll = -(lax.lgamma(count_total + 1.0) - lax.lgamma(bound_total + 1.0) - lax.lgamma(rest_count + 1.0) + bound_total * math.log(PRIOR_RATE) + rest_count * math.log(1.0 - PRIOR_RATE))
    total = jnp.sum(losses) + prior_nll
    return (total / count_total, (total, count_total))

def orthogonal(matrix):
    is_tall = matrix.shape[0] > matrix.shape[1]
    current = matrix.T if is_tall else matrix
    current = current / (jnp.sqrt(jnp.sum(current * current)) + 1e-07)
    for _ in range(5):
        gram_matrix = matmul(current, current.T)
        polynomial = COEF_B * gram_matrix + COEF_C * matmul(gram_matrix, gram_matrix)
        current = COEF_A * current + matmul(polynomial, current)
    return current.T if is_tall else current

def muon(weight, moment, grad):
    new_moment = MOMENTUM * moment + grad
    blend = grad + MOMENTUM * new_moment
    flat = blend.reshape(blend.shape[0], blend.shape[1], -1)
    row_count, col_count = (flat.shape[1], flat.shape[2])
    factor = MUON_RATE * max(1.0, row_count / col_count) ** 0.5
    update = jnp.stack([orthogonal(flat[index]) for index in range(LAYERS)]).reshape(weight.shape)
    return (new_moment, weight * (1.0 - MUON_DECAY) - factor * update)

def adam(weight, first, second, grad, rate, decay):
    first = BETA_ONE * first + (1.0 - BETA_ONE) * grad
    second = BETA_TWO * second + (1.0 - BETA_TWO) * grad * grad
    corrected = first / (1.0 - BETA_ONE ** STEP) / (jnp.sqrt(second / (1.0 - BETA_TWO ** STEP)) + ADAM_EPSILON)
    return (first, second, weight * (1.0 - rate * decay) - rate * corrected)

def reference(tokens, targets, boundaries, lengths, embedding, head, qkv_weight, out_weight, up_weight, up_bias, down_weight, gains, boundary_weight, qkv_moment, out_moment, up_moment, down_moment, embedding_first, embedding_second, head_first, head_second, gains_first, gains_second, bias_first, bias_second, boundary_first, boundary_second):
    counted = (jnp.arange(LEN, dtype=jnp.int32)[None, :] < lengths[:, None]).astype(jnp.float32)
    params = (embedding, head, qkv_weight, out_weight, up_weight, up_bias, down_weight, gains, boundary_weight)
    loss, pullback, aux = jax.vjp(lambda weights: forward(weights, tokens, targets, boundaries, counted), params, has_aux=True)
    grads = pullback(jnp.ones_like(loss))[0]
    squares = sum((jnp.sum(grad * grad) for grad in grads))
    grad_norm = jnp.sqrt(squares)
    factor = jnp.minimum(1.0, CLIP_NORM / (grad_norm + 1e-06))
    g_emb, g_head, g_qkv, g_out, g_up, g_bias, g_down, g_gains, g_bound = [grad * factor for grad in grads]
    qkv_m, qkv_w = muon(qkv_weight, qkv_moment, g_qkv)
    out_m, out_w = muon(out_weight, out_moment, g_out)
    up_m, up_w = muon(up_weight, up_moment, g_up)
    down_m, down_w = muon(down_weight, down_moment, g_down)
    emb_a, emb_b, emb_w = adam(embedding, embedding_first, embedding_second, g_emb, 0.5, 0.1)
    head_a, head_b, head_w = adam(head, head_first, head_second, g_head, 0.05, 0.1)
    gain_a, gain_b, gain_w = adam(gains, gains_first, gains_second, g_gains, 0.6, 0.0)
    bias_a, bias_b, bias_w = adam(up_bias, bias_first, bias_second, g_bias, 0.3, 0.0)
    bound_a, bound_b, bound_w = adam(boundary_weight, boundary_first, boundary_second, g_bound, 0.05, 0.0)
    return (aux[0], aux[1], grad_norm, qkv_m, qkv_w, out_m, out_w, up_m, up_w, down_m, down_w, emb_a, emb_b, emb_w, head_a, head_b, head_w, gain_a, gain_b, gain_w, bias_a, bias_b, bias_w, bound_a, bound_b, bound_w)
```

```python
import math

import jax
import jax.numpy as jnp
from jax import lax
from jax.sharding import Mesh
from jax.sharding import PartitionSpec as P

HEAD_SIZE = 64
VOCAB = 256
LAYERS = 3
SHORT = 160
STEP = 10


NORM_EPSILON = 1e-06
PRIOR_RATE = 0.25
CLIP_NORM = 0.05
MOMENTUM = 0.95
MUON_DECAY = 0.01
MUON_RATE = 4.0
BETA_ONE = 0.9
BETA_TWO = 0.95
ADAM_EPSILON = 1e-08
COEF_A = 3.4445
COEF_B = -4.775
COEF_C = 2.0315


def shortened_2(value):
    return jax.tree.map(lambda a: a.astype(jnp.bfloat16) if a.dtype == jnp.float32 else a, value)


def from_root(value, axis, source):
    kept = jnp.where(lax.axis_index(axis) == source, value, 0).astype(value.dtype)
    return lax.psum(kept, axis)


def matmul_exact(left, right):
    return jnp.dot(left, right, precision=lax.Precision.HIGHEST)


def rms_norm(values, gain_row):
    return (
        values
        * lax.rsqrt(jnp.mean(values * values, axis=-1, keepdims=True) + NORM_EPSILON)
        * gain_row
    )


def block_rows(total):
    return 512 if total % 512 == 0 else total


def causal_scores(queries, key_rows, first_row):
    scores = jnp.einsum(
        "sqhd,skhd->shqk", queries, key_rows, preferred_element_type=jnp.float32
    ) * queries.shape[-1] ** (-0.5)
    row_index = first_row + jnp.arange(queries.shape[1])
    allowed = row_index[:, None] >= jnp.arange(key_rows.shape[1])[None, :]
    return jnp.where(allowed, scores, -1e30)


def attend(queries, key_rows, value_rows):
    total = queries.shape[1]
    step_rows = block_rows(total)
    outputs = []
    summaries = []
    for first_row in range(0, total, step_rows):
        scores = causal_scores(queries[:, first_row : first_row + step_rows], key_rows, first_row)
        highest = jnp.max(scores, axis=-1, keepdims=True)
        expo = jnp.exp(scores - highest)
        totals = jnp.sum(expo, axis=-1, keepdims=True)
        softened = (expo / totals).astype(jnp.bfloat16)
        outputs.append(
            jnp.einsum(
                "shqk,skhd->sqhd", softened, value_rows, preferred_element_type=jnp.float32
            ).astype(jnp.bfloat16)
        )
        summaries.append(highest[..., 0] + jnp.log(totals[..., 0]))
    return (jnp.concatenate(outputs, axis=1), jnp.concatenate(summaries, axis=2))


def attend_back(queries, key_rows, value_rows, grad_mixed, summary):
    total = queries.shape[1]
    step_rows = block_rows(total)
    scale = queries.shape[-1] ** (-0.5)
    grad_keys = jnp.zeros(key_rows.shape, jnp.float32)
    grad_values = jnp.zeros(value_rows.shape, jnp.float32)
    grad_queries = []
    for first_row in range(0, total, step_rows):
        query_block = queries[:, first_row : first_row + step_rows]
        scores = causal_scores(query_block, key_rows, first_row)
        soft = jnp.exp(scores - summary[:, :, first_row : first_row + step_rows, None])
        grad_block = grad_mixed[:, first_row : first_row + step_rows]
        grad_values = grad_values + jnp.einsum(
            "shqk,sqhd->skhd",
            soft.astype(jnp.bfloat16),
            grad_block,
            preferred_element_type=jnp.float32,
        )
        grad_soft = jnp.einsum(
            "sqhd,skhd->shqk", grad_block, value_rows, preferred_element_type=jnp.float32
        )
        centre = jnp.sum(grad_soft * soft, axis=-1, keepdims=True)
        grad_scores = (soft * (grad_soft - centre)).astype(jnp.bfloat16)
        grad_queries.append(
            scale
            * jnp.einsum(
                "shqk,skhd->sqhd", grad_scores, key_rows, preferred_element_type=jnp.float32
            )
        )
        grad_keys = grad_keys + scale * jnp.einsum(
            "shqk,sqhd->skhd", grad_scores, query_block, preferred_element_type=jnp.float32
        )
    return (jnp.concatenate(grad_queries, axis=1), grad_keys, grad_values)


def split_packed(packed, sequences):
    rows_all = packed.shape[0]
    return packed.reshape(
        sequences, rows_all // sequences, 3, packed.shape[2] // HEAD_SIZE, HEAD_SIZE
    )


def layer_forward(inputs, sequences, weights):
    gain_pair, w_qkv, w_out, w_up, b_up, w_down = weights
    rows_all = inputs.shape[0]
    normed = rms_norm(inputs, gain_pair[0]).astype(jnp.bfloat16)
    packed = jnp.einsum(
        "rd,dcf->rcf", normed, w_qkv.astype(jnp.bfloat16), preferred_element_type=jnp.float32
    ).astype(jnp.bfloat16)
    split = split_packed(packed, sequences)
    mixed, summary = attend(split[:, :, 0], split[:, :, 1], split[:, :, 2])
    partial_attn = jnp.dot(
        mixed.reshape(rows_all, -1), w_out.astype(jnp.bfloat16), preferred_element_type=jnp.float32
    )
    after = inputs + lax.psum(partial_attn.astype(jnp.bfloat16), "tensor").astype(jnp.float32)
    normed_ffn = rms_norm(after, gain_pair[1]).astype(jnp.bfloat16)
    hidden = (
        jnp.dot(normed_ffn, w_up.astype(jnp.bfloat16), preferred_element_type=jnp.float32) + b_up
    )
    activated = jax.nn.gelu(hidden).astype(jnp.bfloat16)
    partial_ffn = jnp.dot(
        activated, w_down.astype(jnp.bfloat16), preferred_element_type=jnp.float32
    )
    result = after + lax.psum(partial_ffn.astype(jnp.bfloat16), "tensor").astype(jnp.float32)
    return (result, (inputs, after, packed, mixed, summary, hidden))


def layer_backward(grad_result, saved, sequences, weights):
    gain_pair, w_qkv, w_out, w_up, b_up, w_down = weights
    inputs, after, packed, mixed, summary, hidden = saved
    rows_all = inputs.shape[0]
    grad_branch = grad_result.astype(jnp.bfloat16)
    activated, gelu_back = jax.vjp(jax.nn.gelu, hidden)
    grad_down = jnp.dot(
        activated.astype(jnp.bfloat16).T, grad_branch, preferred_element_type=jnp.float32
    )
    grad_act = jnp.dot(
        grad_branch, w_down.astype(jnp.bfloat16).T, preferred_element_type=jnp.float32
    )
    grad_hidden = gelu_back(grad_act)[0].astype(jnp.bfloat16)
    grad_bias = jnp.sum(grad_hidden.astype(jnp.float32), axis=0)
    normed_ffn, norm_back_two = jax.vjp(rms_norm, after, gain_pair[1])
    grad_up = jnp.dot(
        normed_ffn.astype(jnp.bfloat16).T, grad_hidden, preferred_element_type=jnp.float32
    )
    partial_ffn = jnp.dot(
        grad_hidden, w_up.astype(jnp.bfloat16).T, preferred_element_type=jnp.float32
    )
    grad_normed_ffn = lax.psum(partial_ffn.astype(jnp.bfloat16), "tensor").astype(jnp.float32)
    grad_after_norm, grad_gain_two = norm_back_two(grad_normed_ffn)
    grad_after = grad_result + grad_after_norm
    grad_attn = grad_after.astype(jnp.bfloat16)
    flat_mixed = mixed.reshape(rows_all, -1)
    grad_out = jnp.dot(flat_mixed.T, grad_attn, preferred_element_type=jnp.float32)
    grad_mixed = (
        jnp.dot(grad_attn, w_out.astype(jnp.bfloat16).T, preferred_element_type=jnp.float32)
        .astype(jnp.bfloat16)
        .reshape(mixed.shape)
    )
    split = split_packed(packed, sequences)
    grad_q, grad_k, grad_v = attend_back(
        split[:, :, 0], split[:, :, 1], split[:, :, 2], grad_mixed, summary
    )
    grad_packed = (
        jnp.stack([grad_q, grad_k, grad_v], axis=2).astype(jnp.bfloat16).reshape(rows_all, 3, -1)
    )
    normed, norm_back_one = jax.vjp(rms_norm, inputs, gain_pair[0])
    grad_qkv = jnp.einsum(
        "rd,rcf->dcf", normed.astype(jnp.bfloat16), grad_packed, preferred_element_type=jnp.float32
    )
    partial_attn = jnp.einsum(
        "rcf,dcf->rd", grad_packed, w_qkv.astype(jnp.bfloat16), preferred_element_type=jnp.float32
    )
    grad_normed = lax.psum(partial_attn.astype(jnp.bfloat16), "tensor").astype(jnp.float32)
    grad_inputs_norm, grad_gain_one = norm_back_one(grad_normed)
    grads = (
        jnp.stack([grad_gain_one, grad_gain_two]),
        grad_qkv,
        grad_out,
        grad_up,
        grad_bias,
        grad_down,
    )
    return (grad_after + grad_inputs_norm, grads)


def newton_schulz(matrix):
    is_tall = matrix.shape[0] > matrix.shape[1]
    current = matrix.T if is_tall else matrix
    current = current / (jnp.sqrt(jnp.sum(current * current)) + 1e-07)
    for _ in range(5):
        gram_matrix = matmul_exact(current, current.T)
        polynomial = COEF_B * gram_matrix + COEF_C * matmul_exact(gram_matrix, gram_matrix)
        current = COEF_A * current + matmul_exact(polynomial, current)
    return current.T if is_tall else current


def blank_matrix(matrix):
    return jnp.zeros_like(matrix)


def adam_update(weight, first, second, grad, rate, decay):
    first = BETA_ONE * first + (1.0 - BETA_ONE) * grad
    second = BETA_TWO * second + (1.0 - BETA_TWO) * grad * grad
    corrected = (
        first / (1.0 - BETA_ONE**STEP) / (jnp.sqrt(second / (1.0 - BETA_TWO**STEP)) + ADAM_EPSILON)
    )
    return (first, second, weight * (1.0 - rate * decay) - rate * corrected)


def body(
    tokens,
    targets,
    boundaries,
    lengths,
    embedding,
    head,
    qkv_weight,
    out_weight,
    up_weight,
    up_bias,
    down_weight,
    gains,
    boundary_weight,
    qkv_moment,
    out_moment,
    up_moment,
    down_moment,
    embedding_first,
    embedding_second,
    head_first,
    head_second,
    gains_first,
    gains_second,
    bias_first,
    bias_second,
    boundary_first,
    boundary_second,
):
    sequences, length = tokens.shape
    rows_all = sequences * length
    vocab_ids = jnp.arange(VOCAB, dtype=jnp.int32)
    token_hot = (tokens.reshape(rows_all, 1) == vocab_ids[None, :]).astype(jnp.float32)
    target_hot = (targets.reshape(rows_all, 1) == vocab_ids[None, :]).astype(jnp.float32)
    counted = (
        (jnp.arange(length, dtype=jnp.int32)[None, :] < lengths[:, None])
        .astype(jnp.float32)
        .reshape(rows_all)
    )
    segment = jnp.cumsum(boundaries, axis=1) - boundaries
    short_ids = jnp.arange(SHORT, dtype=jnp.int32)
    pool_hot = (segment[:, None, :] == short_ids[None, :, None]).astype(jnp.bfloat16)
    lift_hot = (segment[:, :, None] - 1 == short_ids[None, None, :]).astype(jnp.bfloat16)
    sizes_seg = jnp.sum(pool_hot.astype(jnp.float32), axis=2, keepdims=True)

    def layer_weights(index):
        return (
            gains[2 * index : 2 * index + 2],
            qkv_weight[index],
            out_weight[index],
            up_weight[index],
            up_bias[index],
            down_weight[index],
        )

    start_rows = matmul_exact(token_hot, embedding)
    first_out, saved_one = layer_forward(start_rows, sequences, layer_weights(0))
    bound_prob = jax.nn.sigmoid(matmul_exact(first_out, boundary_weight))
    first_low = first_out.astype(jnp.bfloat16).reshape(sequences, length, -1)
    shortened = (
        jnp.einsum("sjt,std->sjd", pool_hot, first_low, preferred_element_type=jnp.float32)
        / sizes_seg
    ).reshape(sequences * SHORT, -1)
    short_out, saved_two = layer_forward(shortened, sequences, layer_weights(1))
    short_low = short_out.astype(jnp.bfloat16).reshape(sequences, SHORT, -1)
    lifted = jnp.einsum(
        "stj,sjd->std", lift_hot, short_low, preferred_element_type=jnp.float32
    ).reshape(rows_all, -1)
    final_out, saved_three = layer_forward(first_out + lifted, sequences, layer_weights(2))
    final_norm, final_back = jax.vjp(rms_norm, final_out, gains[2 * LAYERS])
    final_low = final_norm.astype(jnp.bfloat16)
    head_low = head.astype(jnp.bfloat16)
    logits = jnp.dot(final_low, head_low, preferred_element_type=jnp.float32)
    highest = jnp.max(logits, axis=-1, keepdims=True)
    log_probs = (
        logits - highest - jnp.log(jnp.sum(jnp.exp(logits - highest), axis=-1, keepdims=True))
    )
    local_cross = -jnp.sum(counted * jnp.sum(target_hot * log_probs, axis=-1))
    bound_total, count_total, cross_total = lax.psum(
        (jnp.sum(counted * bound_prob), jnp.sum(counted), local_cross), "dp"
    )
    rest_count = count_total - bound_total
    prior_nll = -(
        lax.lgamma(count_total + 1.0)
        - lax.lgamma(bound_total + 1.0)
        - lax.lgamma(rest_count + 1.0)
        + bound_total * math.log(PRIOR_RATE)
        + rest_count * math.log(1.0 - PRIOR_RATE)
    )
    loss_sum = cross_total + prior_nll
    prior_slope = (
        lax.digamma(bound_total + 1.0)
        - lax.digamma(rest_count + 1.0)
        - math.log(PRIOR_RATE)
        + math.log(1.0 - PRIOR_RATE)
    ) / count_total
    grad_logits = ((jnp.exp(log_probs) - target_hot) * (counted / count_total)[:, None]).astype(
        jnp.bfloat16
    )
    grad_head = jnp.dot(final_low.T, grad_logits, preferred_element_type=jnp.float32)
    grad_final, grad_final_gain = final_back(
        jnp.dot(grad_logits, head_low.T, preferred_element_type=jnp.float32)
    )
    grad_merged, grads_three = layer_backward(grad_final, saved_three, sequences, layer_weights(2))
    grad_lift = grad_merged.astype(jnp.bfloat16).reshape(sequences, length, -1)
    grad_short = jnp.einsum(
        "stj,std->sjd", lift_hot, grad_lift, preferred_element_type=jnp.float32
    ).reshape(sequences * SHORT, -1)
    grad_pooled, grads_two = layer_backward(grad_short, saved_two, sequences, layer_weights(1))
    pooled_low = (grad_pooled.reshape(sequences, SHORT, -1) / sizes_seg).astype(jnp.bfloat16)
    prior_term = prior_slope * counted * bound_prob * (1.0 - bound_prob)
    grad_first = (
        grad_merged
        + jnp.einsum(
            "sjt,sjd->std", pool_hot, pooled_low, preferred_element_type=jnp.float32
        ).reshape(rows_all, -1)
        + prior_term[:, None] * boundary_weight[None, :]
    )
    grad_bound = matmul_exact(prior_term, first_out)
    grad_start, grads_one = layer_backward(grad_first, saved_one, sequences, layer_weights(0))
    grad_embed = matmul_exact(token_hot.T, grad_start)
    stacked = [
        jnp.stack([one_part, two_part, three_part])
        for one_part, two_part, three_part in zip(grads_one, grads_two, grads_three)
    ]
    summed = (
        lax.psum(stacked[0].astype(jnp.bfloat16), "dp").astype(jnp.float32),
        lax.psum(stacked[1].astype(jnp.bfloat16), "dp").astype(jnp.float32),
        lax.psum(stacked[2].astype(jnp.bfloat16), "dp").astype(jnp.float32),
        lax.psum(stacked[3].astype(jnp.bfloat16), "dp").astype(jnp.float32),
        lax.psum(stacked[4].astype(jnp.bfloat16), "dp").astype(jnp.float32),
        lax.psum(stacked[5].astype(jnp.bfloat16), "dp").astype(jnp.float32),
        lax.psum(grad_embed.astype(jnp.bfloat16), "dp").astype(jnp.float32),
        lax.psum(grad_head.astype(jnp.bfloat16), "dp").astype(jnp.float32),
        lax.psum(grad_final_gain.astype(jnp.bfloat16), "dp").astype(jnp.float32),
        lax.psum(grad_bound.astype(jnp.bfloat16), "dp").astype(jnp.float32),
    )
    stacked = list(summed[:6])
    grad_embed, grad_head, grad_final_gain, grad_bound = (
        summed[6],
        summed[7],
        summed[8],
        summed[9],
    )
    grad_gains = jnp.concatenate(
        [stacked[0].reshape(2 * LAYERS, -1), grad_final_gain[None, :]], axis=0
    )
    grad_qkv, grad_out, grad_up, grad_bias, grad_down = (
        stacked[1],
        stacked[2],
        stacked[3],
        stacked[4],
        stacked[5],
    )
    split_squares = sum(
        (jnp.sum(grad * grad) for grad in (grad_qkv, grad_out, grad_up, grad_bias, grad_down))
    )
    shared_squares = sum(
        (jnp.sum(grad * grad) for grad in (grad_embed, grad_head, grad_gains, grad_bound))
    )
    grad_norm = jnp.sqrt(lax.psum(split_squares, "tensor") + shared_squares)
    factor = jnp.minimum(1.0, CLIP_NORM / (grad_norm + 1e-06))
    kinds = (
        (qkv_weight, qkv_moment, grad_qkv * factor, 2),
        (out_weight, out_moment, grad_out * factor, 0),
        (up_weight, up_moment, grad_up * factor, 1),
        (down_weight, down_moment, grad_down * factor, 0),
    )
    dp_place = lax.axis_index("dp")
    tensor_place = lax.axis_index("tensor")
    owner_base = lax.axis_size("dp") - 4 * LAYERS
    new_moments = []
    selected = []
    for kind_index in range(4):
        weight, moment, grad, split_dim = kinds[kind_index]
        new_moment = MOMENTUM * moment + grad
        blend = grad + MOMENTUM * new_moment
        chosen = jnp.clip(dp_place - owner_base - kind_index * LAYERS, 0, LAYERS - 1)
        new_moments.append(new_moment)
        selected.append(lax.dynamic_index_in_dim(blend, chosen, 0, keepdims=False))
    gathered = (
        lax.all_gather(selected[0].astype(jnp.bfloat16), "tensor", axis=2, tiled=True).astype(
            jnp.float32
        ),
        lax.all_gather(selected[1].astype(jnp.bfloat16), "tensor", axis=0, tiled=True).astype(
            jnp.float32
        ),
        lax.all_gather(selected[2].astype(jnp.bfloat16), "tensor", axis=1, tiled=True).astype(
            jnp.float32
        ),
        lax.all_gather(selected[3].astype(jnp.bfloat16), "tensor", axis=0, tiled=True).astype(
            jnp.float32
        ),
    )
    own_shards = []
    scales = []
    for kind_index in range(4):
        split_dim = kinds[kind_index][3]
        whole = gathered[kind_index]
        flat = whole.reshape(whole.shape[0], -1)
        first_owner = owner_base + kind_index * LAYERS
        owner = (dp_place >= first_owner) & (dp_place < first_owner + LAYERS)
        ortho = lax.cond(owner, newton_schulz, blank_matrix, flat).reshape(whole.shape)
        width = selected[kind_index].shape[split_dim]
        own_shards.append(
            lax.dynamic_slice_in_dim(ortho, tensor_place * width, width, axis=split_dim)
        )
        scales.append(MUON_RATE * max(1.0, flat.shape[0] / flat.shape[1]) ** 0.5)
    updates = []
    for kind_index in range(4):
        layer_pieces = []
        for layer_index in range(LAYERS):
            layer_pieces.append(
                from_root(
                    shortened_2(own_shards[kind_index]),
                    "dp",
                    owner_base + kind_index * LAYERS + layer_index,
                )
            )
        updates.append(jnp.stack(layer_pieces))
    new_weights = [
        kinds[kind_index][0] * (1.0 - MUON_DECAY) - scales[kind_index] * updates[kind_index]
        for kind_index in range(4)
    ]
    emb_a, emb_b, emb_w = adam_update(
        embedding, embedding_first, embedding_second, grad_embed * factor, 0.5, 0.1
    )
    head_a, head_b, head_w = adam_update(
        head, head_first, head_second, grad_head * factor, 0.05, 0.1
    )
    gain_a, gain_b, gain_w = adam_update(
        gains, gains_first, gains_second, grad_gains * factor, 0.6, 0.0
    )
    bias_a, bias_b, bias_w = adam_update(
        up_bias, bias_first, bias_second, grad_bias * factor, 0.3, 0.0
    )
    bound_a, bound_b, bound_w = adam_update(
        boundary_weight, boundary_first, boundary_second, grad_bound * factor, 0.05, 0.0
    )
    return (
        loss_sum,
        count_total,
        grad_norm,
        new_moments[0],
        new_weights[0],
        new_moments[1],
        new_weights[1],
        new_moments[2],
        new_weights[2],
        new_moments[3],
        new_weights[3],
        emb_a,
        emb_b,
        emb_w,
        head_a,
        head_b,
        head_w,
        gain_a,
        gain_b,
        gain_w,
        bias_a,
        bias_b,
        bias_w,
        bound_a,
        bound_b,
        bound_w,
    )


BF = jnp.bfloat16
F32 = jnp.float32
SWAP = [(0, 1), (1, 0)]
DP_AXES = ("zh", "zl", "y", "core")
HALF_AXES = ("zl", "y", "core", "tensor")
SPLIT_DIMS = (2, 0, 1, 0)


def swap(value, axis):
    return lax.ppermute(value, axis, SWAP)


def summed_over(value, axes):
    for axis in axes:
        value = value + swap(value, axis)
    return value


def tie(values, *tokens):
    return list(lax.optimization_barrier(tuple(values) + tokens)[: len(values)])


def ordered(shard, mine, other, dim):
    return jnp.where(
        shard == 0, jnp.concatenate([mine, other], dim), jnp.concatenate([other, mine], dim)
    )


def exchange_weights(packed, core):
    half = packed.shape[0] // 2
    first = swap(lax.dynamic_slice_in_dim(packed, core * half, half, 0), "tensor")
    second = swap(first, "core")
    return jnp.where(core == 0, jnp.concatenate([first, second]), jnp.concatenate([second, first]))


def attend_local(queries, key_rows, value_rows):
    total = queries.shape[1]
    step = 256 if total % 256 == 0 else total
    outputs, summaries = [], []
    for first in range(0, total, step):
        last = first + step
        scores = (
            jnp.einsum(
                "hqd,hkd->hqk", queries[:, first:last], key_rows[:, :last], preferred_element_type=F32
            )
            * HEAD_SIZE**-0.5
        )
        allowed = (first + jnp.arange(step))[:, None] >= jnp.arange(last)[None, :]
        scores = jnp.where(allowed, scores, -1e30)
        highest = jnp.max(scores, axis=-1, keepdims=True)
        expo = jnp.exp(scores - highest)
        totals = jnp.sum(expo, axis=-1, keepdims=True)
        soft = (expo / totals).astype(BF)
        outputs.append(
            jnp.einsum("hqk,hkd->hqd", soft, value_rows[:, :last], preferred_element_type=F32).astype(BF)
        )
        summaries.append(highest + jnp.log(totals))
    return jnp.concatenate(outputs, axis=1), jnp.concatenate(summaries, axis=1)


def attend_local_back(queries, key_rows, value_rows, grad_mixed, mixed, summary):
    total = queries.shape[1]
    step = 256 if total % 256 == 0 else total
    scale = HEAD_SIZE**-0.5
    centre = jnp.sum(grad_mixed.astype(F32) * mixed.astype(F32), axis=-1, keepdims=True)
    grad_keys = jnp.zeros(key_rows.shape, F32)
    grad_values = jnp.zeros(key_rows.shape, F32)
    grad_queries = []
    for first in range(0, total, step):
        last = first + step
        query_block = queries[:, first:last]
        grad_block = grad_mixed[:, first:last]
        scores = jnp.einsum("hqd,hkd->hqk", query_block, key_rows[:, :last], preferred_element_type=F32) * scale
        allowed = (first + jnp.arange(step))[:, None] >= jnp.arange(last)[None, :]
        soft = jnp.exp(jnp.where(allowed, scores, -1e30) - summary[:, first:last])
        grad_soft = jnp.einsum("hqd,hkd->hqk", grad_block, value_rows[:, :last], preferred_element_type=F32)
        grad_scores = (soft * (grad_soft - centre[:, first:last])).astype(BF)
        grad_queries.append(
            scale * jnp.einsum("hqk,hkd->hqd", grad_scores, key_rows[:, :last], preferred_element_type=F32)
        )
        new_keys = scale * jnp.einsum("hqk,hqd->hkd", grad_scores, query_block, preferred_element_type=F32)
        new_values = jnp.einsum("hqk,hqd->hkd", soft.astype(BF), grad_block, preferred_element_type=F32)
        pad = ((0, 0), (0, total - last), (0, 0))
        grad_keys = grad_keys + jnp.pad(new_keys, pad)
        grad_values = grad_values + jnp.pad(new_values, pad)
    return jnp.concatenate(grad_queries, axis=1), grad_keys, grad_values


def heads_first(rows):
    return jnp.transpose(rows.reshape(rows.shape[0], -1, HEAD_SIZE), (1, 0, 2))


def rows_first(values):
    return jnp.transpose(values, (1, 0, 2)).reshape(values.shape[1], -1)


def whole_layer_forward(inputs, weights):
    gain_pair, w_qkv, w_out, w_up, b_up, w_down = weights
    normed = rms_norm(inputs, gain_pair[0]).astype(BF)
    packed = [
        heads_first(jnp.dot(normed, w_qkv[part], preferred_element_type=F32).astype(BF)) for part in range(3)
    ]
    mixed, summary = attend_local(*packed)
    after = inputs + jnp.dot(rows_first(mixed), w_out, preferred_element_type=F32)
    normed_ffn = rms_norm(after, gain_pair[1]).astype(BF)
    hidden = jnp.dot(normed_ffn, w_up, preferred_element_type=F32) + b_up
    result = after + jnp.dot(jax.nn.gelu(hidden).astype(BF), w_down, preferred_element_type=F32)
    return result, (inputs, after, packed, mixed, summary, hidden)


def whole_layer_backward(grad_result, saved, weights):
    gain_pair, w_qkv, w_out, w_up, b_up, w_down = weights
    inputs, after, packed, mixed, summary, hidden = saved
    grad_branch = grad_result.astype(BF)
    activated, gelu_back = jax.vjp(jax.nn.gelu, hidden)
    grad_down = jnp.dot(activated.astype(BF).T, grad_branch, preferred_element_type=F32)
    grad_act = jnp.dot(grad_branch, w_down.T, preferred_element_type=F32)
    grad_hidden = gelu_back(grad_act)[0].astype(BF)
    grad_bias = jnp.sum(grad_hidden.astype(F32), axis=0)
    normed_ffn, norm_back_two = jax.vjp(rms_norm, after, gain_pair[1])
    grad_up = jnp.dot(normed_ffn.astype(BF).T, grad_hidden, preferred_element_type=F32)
    grad_after_norm, grad_gain_two = norm_back_two(jnp.dot(grad_hidden, w_up.T, preferred_element_type=F32))
    grad_after = grad_result + grad_after_norm
    grad_attn = grad_after.astype(BF)
    grad_out = jnp.dot(rows_first(mixed).T, grad_attn, preferred_element_type=F32)
    grad_mixed = heads_first(jnp.dot(grad_attn, w_out.T, preferred_element_type=F32).astype(BF))
    grad_parts = [
        rows_first(part.astype(BF)) for part in attend_local_back(*packed, grad_mixed, mixed, summary)
    ]
    normed, norm_back_one = jax.vjp(rms_norm, inputs, gain_pair[0])
    normed_low = normed.astype(BF)
    grad_qkv = jnp.stack([jnp.dot(normed_low.T, part, preferred_element_type=F32) for part in grad_parts])
    grad_normed = sum(
        jnp.dot(part, w_qkv[at].T, preferred_element_type=F32) for at, part in enumerate(grad_parts)
    )
    grad_inputs_norm, grad_gain_one = norm_back_one(grad_normed)
    grads = (jnp.stack([grad_gain_one, grad_gain_two]), grad_qkv, grad_out, grad_up, grad_bias, grad_down)
    return grad_after + grad_inputs_norm, grads


def shard_pair(shard, values, dim):
    width = values.shape[dim] // 2
    mine = lax.dynamic_slice_in_dim(values, shard * width, width, dim)
    return mine, lax.dynamic_slice_in_dim(values, (1 - shard) * width, width, dim)


def to_rows(qkv, out, up, down):
    ups = [up[:, :512], up[:, 512:]]
    qkvs = [qkv.reshape(768, 512)]
    return jnp.concatenate([out, down] + ups + qkvs, axis=0)


def from_rows(rows):
    up = jnp.concatenate([rows[1280:1792], rows[1792:2304]], axis=1)
    return rows[2304:3072].reshape(3, 512, 256), rows[0:256], up, rows[256:1280]


def newton_map(gram):
    inverse = 1.0 / (jnp.sqrt(jnp.trace(gram)) + 1e-07)
    gram = gram * (inverse * inverse)
    eye = jnp.eye(512, dtype=F32)
    total = None
    for index in range(5):
        poly = COEF_A * eye + COEF_B * gram + COEF_C * matmul_exact(gram, gram)
        total = poly if total is None else matmul_exact(total, poly)
        if index < 4:
            gram = matmul_exact(matmul_exact(gram, poly), poly)
            gram = 0.5 * (gram + gram.T)
    return (total * inverse).astype(BF)


def gram_of(left, right, dims):
    return lax.dot_general(left, right, (dims, ((), ())), preferred_element_type=F32)


def sequence_body(
    tokens, targets, boundaries, lengths, embedding, head, qkv_weight, out_weight, up_weight, up_bias,
    down_weight, gains, boundary_weight, qkv_moment, out_moment, up_moment, down_moment, embedding_first,
    embedding_second, head_first, head_second, gains_first, gains_second, bias_first, bias_second,
    boundary_first, boundary_second,
):
    length = tokens.shape[1]
    core, shard = lax.axis_index("core"), lax.axis_index("tensor")
    place_y, place_zl = lax.axis_index("y"), lax.axis_index("zl")
    own_length = lax.dynamic_index_in_dim(lengths, shard, 0, keepdims=False)
    token_row = lax.dynamic_index_in_dim(tokens, shard, 0, keepdims=False)
    target_row = lax.dynamic_index_in_dim(targets, shard, 0, keepdims=False)
    bound_row = lax.dynamic_index_in_dim(boundaries, shard, 0, keepdims=False)
    qkv_parts = jnp.transpose(qkv_weight, (0, 2, 1, 3))
    vocab_ids = jnp.arange(VOCAB, dtype=jnp.int32)
    target_hot = (target_row[:, None] == vocab_ids[None, :]).astype(F32)
    counted = (jnp.arange(length, dtype=jnp.int32) < own_length).astype(F32)
    segment = jnp.cumsum(bound_row) - bound_row
    short_ids = jnp.arange(SHORT, dtype=jnp.int32)
    pool_hot = (segment[None, :] == short_ids[:, None]).astype(BF)
    lift_hot = (segment[:, None] - 1 == short_ids[None, :]).astype(BF)
    sizes_seg = jnp.sum(pool_hot.astype(F32), axis=1, keepdims=True)

    rows_own, rows_other = [], []
    for layer in range(LAYERS):
        packed = to_rows(
            *[value[layer].astype(BF) for value in (qkv_parts, out_weight, up_weight, down_weight)]
        )
        if rows_other:
            (packed,) = tie([packed], rows_other[-1])
        rows_own.append(packed)
        rows_other.append(exchange_weights(packed, core))
    bias_other = swap(up_bias, "tensor")
    bias_whole = ordered(shard, up_bias, bias_other, 1)

    def layer_weights(layer):
        mine, other = from_rows(rows_own[layer]), from_rows(rows_other[layer])
        dims = (2, 0, 1, 0)
        w_qkv, w_out, w_up, w_down = [
            ordered(shard, own, far, dim) for own, far, dim in zip(mine, other, dims)
        ]
        return gains[2 * layer : 2 * layer + 2], w_qkv, w_out, w_up, bias_whole[layer], w_down

    weights = [layer_weights(layer) for layer in range(LAYERS)]
    wide = jnp.zeros((8, 128), F32)
    count_total = summed_over(
        jnp.sum(jnp.clip(lengths, 0, length)).astype(F32).reshape(1, 1) + wide, DP_AXES
    )[0, 0]

    token_hot = (token_row[:, None] == vocab_ids[None, :]).astype(BF)
    table_high = embedding.astype(BF)
    table_rest = embedding - table_high.astype(F32)
    table_mid = table_rest.astype(BF)
    table_low = (table_rest - table_mid.astype(F32)).astype(BF)
    start_rows = sum(
        jnp.dot(token_hot, part, preferred_element_type=F32) for part in (table_high, table_mid, table_low)
    )
    first_out, saved_one = whole_layer_forward(start_rows, weights[0])
    bound_prob = jax.nn.sigmoid(jnp.sum(first_out * boundary_weight, axis=-1))
    shortened = jnp.dot(pool_hot, first_out.astype(BF), preferred_element_type=F32) / sizes_seg
    short_out, saved_two = whole_layer_forward(shortened, weights[1])
    lifted = jnp.dot(lift_hot, short_out.astype(BF), preferred_element_type=F32)
    final_out, saved_three = whole_layer_forward(first_out + lifted, weights[2])
    bound_total = summed_over(jnp.sum(counted * bound_prob).reshape(1, 1) + wide, DP_AXES + ("tensor",))[0, 0]
    final_norm, final_back = jax.vjp(rms_norm, final_out, gains[2 * LAYERS])
    final_low = final_norm.astype(BF)
    head_low = head.astype(BF)
    logits = jnp.dot(final_low, head_low, preferred_element_type=F32)
    highest = jnp.max(logits, axis=-1, keepdims=True)
    log_probs = logits - highest - jnp.log(jnp.sum(jnp.exp(logits - highest), axis=-1, keepdims=True))
    local_cross = -jnp.sum(counted * jnp.sum(target_hot * log_probs, axis=-1))
    rest_count = count_total - bound_total
    prior_nll = -(
        lax.lgamma(count_total + 1.0)
        - lax.lgamma(bound_total + 1.0)
        - lax.lgamma(rest_count + 1.0)
        + bound_total * math.log(PRIOR_RATE)
        + rest_count * math.log(1.0 - PRIOR_RATE)
    )
    prior_slope = (
        lax.digamma(bound_total + 1.0)
        - lax.digamma(rest_count + 1.0)
        - math.log(PRIOR_RATE)
        + math.log(1.0 - PRIOR_RATE)
    ) / count_total
    grad_logits = ((jnp.exp(log_probs) - target_hot) * (counted / count_total)[:, None]).astype(BF)
    grad_head = jnp.dot(final_low.T, grad_logits, preferred_element_type=F32)
    grad_final, gain_final = final_back(jnp.dot(grad_logits, head_low.T, preferred_element_type=F32))

    def reduce_layer(grads):
        _, grad_qkv, grad_out, grad_up, _, grad_down = grads
        pairs = [
            shard_pair(shard, value.astype(BF), dim)
            for value, dim in zip((grad_qkv, grad_out, grad_up, grad_down), SPLIT_DIMS)
        ]
        mine = to_rows(*[pair[0] for pair in pairs])
        other = to_rows(*[pair[1] for pair in pairs])
        half = mine.shape[0] // 2
        kept = [lax.dynamic_slice_in_dim(value, core * half, half, 0) for value in (mine, other)]
        sent = [lax.dynamic_slice_in_dim(value, (1 - core) * half, half, 0) for value in (mine, other)]
        got = swap(jnp.stack(sent), "core")
        send_x = (kept[1].astype(F32) + got[1].astype(F32)).astype(BF)
        total = kept[0].astype(F32) + got[0].astype(F32) + swap(send_x, "tensor").astype(F32)
        return total.astype(BF)

    grad_merged, grads_three = whole_layer_backward(grad_final, saved_three, weights[2])
    sums = [None, None, reduce_layer(grads_three)]
    grad_short = jnp.dot(lift_hot.T, grad_merged.astype(BF), preferred_element_type=F32)
    grad_pooled, grads_two = whole_layer_backward(grad_short, saved_two, weights[1])
    sums[1] = reduce_layer(grads_two)
    early = lax.psum(jnp.stack([sums[1], sums[2]]), ("zh", "zl", "y"))
    pooled_low = (grad_pooled / sizes_seg).astype(BF)
    prior_term = prior_slope * counted * bound_prob * (1.0 - bound_prob)
    grad_first = (
        grad_merged
        + jnp.dot(pool_hot.T, pooled_low, preferred_element_type=F32)
        + prior_term[:, None] * boundary_weight[None, :]
    )
    grad_bound = jnp.sum(prior_term[:, None] * first_out, axis=0)
    grad_start, grads_one = whole_layer_backward(grad_first, saved_one, weights[0])
    start_high = grad_start.astype(BF)
    start_low = (grad_start - start_high.astype(F32)).astype(BF)
    grad_embed = sum(jnp.dot(token_hot.T, part, preferred_element_type=F32) for part in (start_high, start_low))
    sums[0] = reduce_layer(grads_one)
    tables = jnp.concatenate([grad_embed.reshape(256, 512), grad_head.reshape(256, 512)], axis=0).astype(BF)
    tables = (tables.astype(F32) + swap(tables, "tensor").astype(F32)).astype(BF)
    tables = (tables.astype(F32) + swap(tables, "core").astype(F32)).astype(BF)
    late = lax.psum(jnp.concatenate([sums[0], tables], axis=0), ("zh", "zl", "y"))
    halves = [late[:1536], early[0], early[1]]
    stacked = jnp.stack(halves)
    other_halves = swap(stacked, "core")
    rows = jnp.where(
        core == 0,
        jnp.concatenate([stacked, other_halves], axis=1),
        jnp.concatenate([other_halves, stacked], axis=1),
    )
    grad_embed, grad_head = late[1536:1792].astype(F32), late[1792:2048].reshape(512, 256).astype(F32)
    split = [from_rows(rows[layer]) for layer in range(LAYERS)]
    grads = [jnp.stack([split[layer][kind] for layer in range(LAYERS)]).astype(F32) for kind in range(4)]

    all_grads = (grads_one, grads_two, grads_three)
    bias_pairs = jnp.stack([each[4] for each in all_grads])
    vectors = jnp.concatenate(
        [each[0] for each in all_grads]
        + [gain_final[None, :], grad_bound[None, :], bias_pairs.reshape(12, 512)]
        + [jnp.broadcast_to(local_cross.reshape(1, 1), (4, 512))],
        axis=0,
    )
    vectors = summed_over(vectors, DP_AXES + ("tensor",))
    grad_gains, grad_bound, both_biases = vectors[0:7], vectors[7], vectors[8:20].reshape(LAYERS, 2048)
    loss_sum = vectors[20, 0] + prior_nll
    grad_bias = lax.dynamic_slice_in_dim(both_biases, shard * 1024, 1024, 1)
    shared_squares = (
        jnp.sum(vectors[0:20] * vectors[0:20]) + jnp.sum(grad_embed * grad_embed) + jnp.sum(grad_head * grad_head)
    )
    split_squares = sum(jnp.sum(grad * grad) for grad in grads)
    split_squares = summed_over(split_squares.reshape(1, 1) + wide, ("tensor",))[0, 0]
    grad_norm = jnp.sqrt(split_squares + shared_squares)
    factor = jnp.minimum(1.0, CLIP_NORM / (grad_norm + 1e-06))

    moments = [jnp.transpose(qkv_moment, (0, 2, 1, 3)), out_moment, up_moment, down_moment]
    new_moments = [MOMENTUM * moment + grad * factor for moment, grad in zip(moments, grads)]
    blends = [
        (grad * factor + MOMENTUM * new).astype(BF) for grad, new in zip(grads, new_moments)
    ]
    slot = jnp.minimum(((place_zl * 2 + place_y) * 2 + core) * 2 + shard, 4 * LAYERS - 1)
    own_layer = slot // 4
    chosen = [lax.dynamic_index_in_dim(blend, own_layer, 0, keepdims=False) for blend in blends]

    def first_pair(values):
        qkv, out, up, down = values
        gram = sum(gram_of(qkv[part], qkv[part], ((1,), (1,))) for part in range(3))
        return jnp.stack([gram, gram_of(out, out, ((0,), (0,)))])

    def second_pair(values):
        qkv, out, up, down = values
        return jnp.stack([gram_of(up, up, ((1,), (1,))), gram_of(down, down, ((0,), (0,)))])

    shares = lax.cond((slot // 2) % 2 == 0, first_pair, second_pair, chosen)
    sent = swap(lax.dynamic_index_in_dim(shares, 1 - shard, 0, keepdims=False), "tensor")
    kept = lax.dynamic_index_in_dim(shares, shard, 0, keepdims=False)
    maps = lax.all_gather(newton_map(kept + sent), HALF_AXES, axis=0, tiled=False)
    weights_in = [qkv_parts, out_weight, up_weight, down_weight]
    new_weights = [[] for _ in range(4)]
    for layer in range(LAYERS):
        qkv, out, up, down = [blend[layer] for blend in blends]
        at = 4 * layer
        updates = [
            jnp.stack([jnp.dot(maps[at], qkv[part], preferred_element_type=F32) for part in range(3)]),
            jnp.dot(out, maps[at + 1], preferred_element_type=F32),
            jnp.dot(maps[at + 2], up, preferred_element_type=F32),
            2.0 * jnp.dot(down, maps[at + 3], preferred_element_type=F32),
        ]
        for kind in range(4):
            new_weights[kind].append(
                weights_in[kind][layer] * (1.0 - MUON_DECAY) - MUON_RATE * updates[kind]
            )
    new_weights = [jnp.stack(value) for value in new_weights]
    new_moments[0] = jnp.transpose(new_moments[0], (0, 2, 1, 3))
    new_weights[0] = jnp.transpose(new_weights[0], (0, 2, 1, 3))
    muon = []
    for new_moment, new_weight in zip(new_moments, new_weights):
        muon += [new_moment, new_weight]
    return (
        loss_sum,
        count_total,
        grad_norm,
        *muon,
        *adam_update(embedding, embedding_first, embedding_second, grad_embed * factor, 0.5, 0.1),
        *adam_update(head, head_first, head_second, grad_head * factor, 0.05, 0.1),
        *adam_update(gains, gains_first, gains_second, grad_gains * factor, 0.6, 0.0),
        *adam_update(up_bias, bias_first, bias_second, grad_bias * factor, 0.3, 0.0),
        *adam_update(boundary_weight, boundary_first, boundary_second, grad_bound * factor, 0.05, 0.0),
    )


def sequence_specs(dp):
    split = [P(None, None, None, "tensor"), P(None, "tensor", None), P(None, None, "tensor"), P(None, "tensor"), P(None, "tensor", None)]
    ins = [P(dp, None)] * 3 + [P(dp), P(), P()] + split + [P(), P()]
    ins += [split[0], split[1], split[2], split[4]] + [P()] * 6 + [split[3]] * 2 + [P()] * 2
    outs = [P()] * 3
    for kind in (0, 1, 2, 4):
        outs += [split[kind]] * 2
    outs += [P()] * 9 + [split[3]] * 3 + [P()] * 3
    return tuple(ins), tuple(outs)


def solution(mesh):
    def run(tokens, *rest):
        dp, tensor = mesh.shape["dp"], mesh.shape["tensor"]
        if (dp, tensor) == (16, 2) and tokens.shape[0] == tensor * dp:
            parts = Mesh(mesh.devices.reshape(2, 2, 2, 2, 2), DP_AXES + ("tensor",))
            ins, outs = sequence_specs(DP_AXES)
            step = jax.shard_map(sequence_body, mesh=parts, in_specs=ins, out_specs=outs, check_vma=False)
        else:
            ins, outs = sequence_specs("dp")
            step = jax.shard_map(body, mesh=mesh, in_specs=ins, out_specs=outs, check_vma=False)
        return step(tokens, *rest)

    return run
```

```python
import math

import jax
import jax.numpy as jnp
from jax import lax
from jax.sharding import Mesh
from jax.sharding import PartitionSpec as P

HEAD_SIZE = 64
VOCAB = 256
LAYERS = 3
SHORT = 160
STEP = 10


NORM_EPSILON = 1e-06
PRIOR_RATE = 0.25
CLIP_NORM = 0.05
MOMENTUM = 0.95
MUON_DECAY = 0.01
MUON_RATE = 4.0
BETA_ONE = 0.9
BETA_TWO = 0.95
ADAM_EPSILON = 1e-08
COEF_A = 3.4445
COEF_B = -4.775
COEF_C = 2.0315


def shortened_2(value):
    return jax.tree.map(lambda a: a.astype(jnp.bfloat16) if a.dtype == jnp.float32 else a, value)


def from_root(value, axis, source):
    kept = jnp.where(lax.axis_index(axis) == source, value, 0).astype(value.dtype)
    return lax.psum(kept, axis)


def matmul_exact(left, right):
    return jnp.dot(left, right, precision=lax.Precision.HIGHEST)


def rms_norm(values, gain_row):
    return (
        values
        * lax.rsqrt(jnp.mean(values * values, axis=-1, keepdims=True) + NORM_EPSILON)
        * gain_row
    )


def block_rows(total):
    return 512 if total % 512 == 0 else total


def causal_scores(queries, key_rows, first_row):
    scores = jnp.einsum(
        "sqhd,skhd->shqk", queries, key_rows, preferred_element_type=jnp.float32
    ) * queries.shape[-1] ** (-0.5)
    row_index = first_row + jnp.arange(queries.shape[1])
    allowed = row_index[:, None] >= jnp.arange(key_rows.shape[1])[None, :]
    return jnp.where(allowed, scores, -1e30)


def attend(queries, key_rows, value_rows):
    total = queries.shape[1]
    step_rows = block_rows(total)
    outputs = []
    summaries = []
    for first_row in range(0, total, step_rows):
        scores = causal_scores(queries[:, first_row : first_row + step_rows], key_rows, first_row)
        highest = jnp.max(scores, axis=-1, keepdims=True)
        expo = jnp.exp(scores - highest)
        totals = jnp.sum(expo, axis=-1, keepdims=True)
        softened = (expo / totals).astype(jnp.bfloat16)
        outputs.append(
            jnp.einsum(
                "shqk,skhd->sqhd", softened, value_rows, preferred_element_type=jnp.float32
            ).astype(jnp.bfloat16)
        )
        summaries.append(highest[..., 0] + jnp.log(totals[..., 0]))
    return (jnp.concatenate(outputs, axis=1), jnp.concatenate(summaries, axis=2))


def attend_back(queries, key_rows, value_rows, grad_mixed, summary):
    total = queries.shape[1]
    step_rows = block_rows(total)
    scale = queries.shape[-1] ** (-0.5)
    grad_keys = jnp.zeros(key_rows.shape, jnp.float32)
    grad_values = jnp.zeros(value_rows.shape, jnp.float32)
    grad_queries = []
    for first_row in range(0, total, step_rows):
        query_block = queries[:, first_row : first_row + step_rows]
        scores = causal_scores(query_block, key_rows, first_row)
        soft = jnp.exp(scores - summary[:, :, first_row : first_row + step_rows, None])
        grad_block = grad_mixed[:, first_row : first_row + step_rows]
        grad_values = grad_values + jnp.einsum(
            "shqk,sqhd->skhd",
            soft.astype(jnp.bfloat16),
            grad_block,
            preferred_element_type=jnp.float32,
        )
        grad_soft = jnp.einsum(
            "sqhd,skhd->shqk", grad_block, value_rows, preferred_element_type=jnp.float32
        )
        centre = jnp.sum(grad_soft * soft, axis=-1, keepdims=True)
        grad_scores = (soft * (grad_soft - centre)).astype(jnp.bfloat16)
        grad_queries.append(
            scale
            * jnp.einsum(
                "shqk,skhd->sqhd", grad_scores, key_rows, preferred_element_type=jnp.float32
            )
        )
        grad_keys = grad_keys + scale * jnp.einsum(
            "shqk,sqhd->skhd", grad_scores, query_block, preferred_element_type=jnp.float32
        )
    return (jnp.concatenate(grad_queries, axis=1), grad_keys, grad_values)


def split_packed(packed, sequences):
    rows_all = packed.shape[0]
    return packed.reshape(
        sequences, rows_all // sequences, 3, packed.shape[2] // HEAD_SIZE, HEAD_SIZE
    )


def layer_forward(inputs, sequences, weights):
    gain_pair, w_qkv, w_out, w_up, b_up, w_down = weights
    rows_all = inputs.shape[0]
    normed = rms_norm(inputs, gain_pair[0]).astype(jnp.bfloat16)
    packed = jnp.einsum(
        "rd,dcf->rcf", normed, w_qkv.astype(jnp.bfloat16), preferred_element_type=jnp.float32
    ).astype(jnp.bfloat16)
    split = split_packed(packed, sequences)
    mixed, summary = attend(split[:, :, 0], split[:, :, 1], split[:, :, 2])
    partial_attn = jnp.dot(
        mixed.reshape(rows_all, -1), w_out.astype(jnp.bfloat16), preferred_element_type=jnp.float32
    )
    after = inputs + lax.psum(partial_attn.astype(jnp.bfloat16), "tensor").astype(jnp.float32)
    normed_ffn = rms_norm(after, gain_pair[1]).astype(jnp.bfloat16)
    hidden = (
        jnp.dot(normed_ffn, w_up.astype(jnp.bfloat16), preferred_element_type=jnp.float32) + b_up
    )
    activated = jax.nn.gelu(hidden).astype(jnp.bfloat16)
    partial_ffn = jnp.dot(
        activated, w_down.astype(jnp.bfloat16), preferred_element_type=jnp.float32
    )
    result = after + lax.psum(partial_ffn.astype(jnp.bfloat16), "tensor").astype(jnp.float32)
    return (result, (inputs, after, packed, mixed, summary, hidden))


def layer_backward(grad_result, saved, sequences, weights):
    gain_pair, w_qkv, w_out, w_up, b_up, w_down = weights
    inputs, after, packed, mixed, summary, hidden = saved
    rows_all = inputs.shape[0]
    grad_branch = grad_result.astype(jnp.bfloat16)
    activated, gelu_back = jax.vjp(jax.nn.gelu, hidden)
    grad_down = jnp.dot(
        activated.astype(jnp.bfloat16).T, grad_branch, preferred_element_type=jnp.float32
    )
    grad_act = jnp.dot(
        grad_branch, w_down.astype(jnp.bfloat16).T, preferred_element_type=jnp.float32
    )
    grad_hidden = gelu_back(grad_act)[0].astype(jnp.bfloat16)
    grad_bias = jnp.sum(grad_hidden.astype(jnp.float32), axis=0)
    normed_ffn, norm_back_two = jax.vjp(rms_norm, after, gain_pair[1])
    grad_up = jnp.dot(
        normed_ffn.astype(jnp.bfloat16).T, grad_hidden, preferred_element_type=jnp.float32
    )
    partial_ffn = jnp.dot(
        grad_hidden, w_up.astype(jnp.bfloat16).T, preferred_element_type=jnp.float32
    )
    grad_normed_ffn = lax.psum(partial_ffn.astype(jnp.bfloat16), "tensor").astype(jnp.float32)
    grad_after_norm, grad_gain_two = norm_back_two(grad_normed_ffn)
    grad_after = grad_result + grad_after_norm
    grad_attn = grad_after.astype(jnp.bfloat16)
    flat_mixed = mixed.reshape(rows_all, -1)
    grad_out = jnp.dot(flat_mixed.T, grad_attn, preferred_element_type=jnp.float32)
    grad_mixed = (
        jnp.dot(grad_attn, w_out.astype(jnp.bfloat16).T, preferred_element_type=jnp.float32)
        .astype(jnp.bfloat16)
        .reshape(mixed.shape)
    )
    split = split_packed(packed, sequences)
    grad_q, grad_k, grad_v = attend_back(
        split[:, :, 0], split[:, :, 1], split[:, :, 2], grad_mixed, summary
    )
    grad_packed = (
        jnp.stack([grad_q, grad_k, grad_v], axis=2).astype(jnp.bfloat16).reshape(rows_all, 3, -1)
    )
    normed, norm_back_one = jax.vjp(rms_norm, inputs, gain_pair[0])
    grad_qkv = jnp.einsum(
        "rd,rcf->dcf", normed.astype(jnp.bfloat16), grad_packed, preferred_element_type=jnp.float32
    )
    partial_attn = jnp.einsum(
        "rcf,dcf->rd", grad_packed, w_qkv.astype(jnp.bfloat16), preferred_element_type=jnp.float32
    )
    grad_normed = lax.psum(partial_attn.astype(jnp.bfloat16), "tensor").astype(jnp.float32)
    grad_inputs_norm, grad_gain_one = norm_back_one(grad_normed)
    grads = (
        jnp.stack([grad_gain_one, grad_gain_two]),
        grad_qkv,
        grad_out,
        grad_up,
        grad_bias,
        grad_down,
    )
    return (grad_after + grad_inputs_norm, grads)


def newton_schulz(matrix):
    is_tall = matrix.shape[0] > matrix.shape[1]
    current = matrix.T if is_tall else matrix
    current = current / (jnp.sqrt(jnp.sum(current * current)) + 1e-07)
    for _ in range(5):
        gram_matrix = matmul_exact(current, current.T)
        polynomial = COEF_B * gram_matrix + COEF_C * matmul_exact(gram_matrix, gram_matrix)
        current = COEF_A * current + matmul_exact(polynomial, current)
    return current.T if is_tall else current


def blank_matrix(matrix):
    return jnp.zeros_like(matrix)


def adam_update(weight, first, second, grad, rate, decay):
    first = BETA_ONE * first + (1.0 - BETA_ONE) * grad
    second = BETA_TWO * second + (1.0 - BETA_TWO) * grad * grad
    corrected = (
        first / (1.0 - BETA_ONE**STEP) / (jnp.sqrt(second / (1.0 - BETA_TWO**STEP)) + ADAM_EPSILON)
    )
    return (first, second, weight * (1.0 - rate * decay) - rate * corrected)


def body(
    tokens,
    targets,
    boundaries,
    lengths,
    embedding,
    head,
    qkv_weight,
    out_weight,
    up_weight,
    up_bias,
    down_weight,
    gains,
    boundary_weight,
    qkv_moment,
    out_moment,
    up_moment,
    down_moment,
    embedding_first,
    embedding_second,
    head_first,
    head_second,
    gains_first,
    gains_second,
    bias_first,
    bias_second,
    boundary_first,
    boundary_second,
):
    sequences, length = tokens.shape
    rows_all = sequences * length
    vocab_ids = jnp.arange(VOCAB, dtype=jnp.int32)
    token_hot = (tokens.reshape(rows_all, 1) == vocab_ids[None, :]).astype(jnp.float32)
    target_hot = (targets.reshape(rows_all, 1) == vocab_ids[None, :]).astype(jnp.float32)
    counted = (
        (jnp.arange(length, dtype=jnp.int32)[None, :] < lengths[:, None])
        .astype(jnp.float32)
        .reshape(rows_all)
    )
    segment = jnp.cumsum(boundaries, axis=1) - boundaries
    short_ids = jnp.arange(SHORT, dtype=jnp.int32)
    pool_hot = (segment[:, None, :] == short_ids[None, :, None]).astype(jnp.bfloat16)
    lift_hot = (segment[:, :, None] - 1 == short_ids[None, None, :]).astype(jnp.bfloat16)
    sizes_seg = jnp.sum(pool_hot.astype(jnp.float32), axis=2, keepdims=True)

    def layer_weights(index):
        return (
            gains[2 * index : 2 * index + 2],
            qkv_weight[index],
            out_weight[index],
            up_weight[index],
            up_bias[index],
            down_weight[index],
        )

    start_rows = matmul_exact(token_hot, embedding)
    first_out, saved_one = layer_forward(start_rows, sequences, layer_weights(0))
    bound_prob = jax.nn.sigmoid(matmul_exact(first_out, boundary_weight))
    first_low = first_out.astype(jnp.bfloat16).reshape(sequences, length, -1)
    shortened = (
        jnp.einsum("sjt,std->sjd", pool_hot, first_low, preferred_element_type=jnp.float32)
        / sizes_seg
    ).reshape(sequences * SHORT, -1)
    short_out, saved_two = layer_forward(shortened, sequences, layer_weights(1))
    short_low = short_out.astype(jnp.bfloat16).reshape(sequences, SHORT, -1)
    lifted = jnp.einsum(
        "stj,sjd->std", lift_hot, short_low, preferred_element_type=jnp.float32
    ).reshape(rows_all, -1)
    final_out, saved_three = layer_forward(first_out + lifted, sequences, layer_weights(2))
    final_norm, final_back = jax.vjp(rms_norm, final_out, gains[2 * LAYERS])
    final_low = final_norm.astype(jnp.bfloat16)
    head_low = head.astype(jnp.bfloat16)
    logits = jnp.dot(final_low, head_low, preferred_element_type=jnp.float32)
    highest = jnp.max(logits, axis=-1, keepdims=True)
    log_probs = (
        logits - highest - jnp.log(jnp.sum(jnp.exp(logits - highest), axis=-1, keepdims=True))
    )
    local_cross = -jnp.sum(counted * jnp.sum(target_hot * log_probs, axis=-1))
    bound_total, count_total, cross_total = lax.psum(
        (jnp.sum(counted * bound_prob), jnp.sum(counted), local_cross), "dp"
    )
    rest_count = count_total - bound_total
    prior_nll = -(
        lax.lgamma(count_total + 1.0)
        - lax.lgamma(bound_total + 1.0)
        - lax.lgamma(rest_count + 1.0)
        + bound_total * math.log(PRIOR_RATE)
        + rest_count * math.log(1.0 - PRIOR_RATE)
    )
    loss_sum = cross_total + prior_nll
    prior_slope = (
        lax.digamma(bound_total + 1.0)
        - lax.digamma(rest_count + 1.0)
        - math.log(PRIOR_RATE)
        + math.log(1.0 - PRIOR_RATE)
    ) / count_total
    grad_logits = ((jnp.exp(log_probs) - target_hot) * (counted / count_total)[:, None]).astype(
        jnp.bfloat16
    )
    grad_head = jnp.dot(final_low.T, grad_logits, preferred_element_type=jnp.float32)
    grad_final, grad_final_gain = final_back(
        jnp.dot(grad_logits, head_low.T, preferred_element_type=jnp.float32)
    )
    grad_merged, grads_three = layer_backward(grad_final, saved_three, sequences, layer_weights(2))
    grad_lift = grad_merged.astype(jnp.bfloat16).reshape(sequences, length, -1)
    grad_short = jnp.einsum(
        "stj,std->sjd", lift_hot, grad_lift, preferred_element_type=jnp.float32
    ).reshape(sequences * SHORT, -1)
    grad_pooled, grads_two = layer_backward(grad_short, saved_two, sequences, layer_weights(1))
    pooled_low = (grad_pooled.reshape(sequences, SHORT, -1) / sizes_seg).astype(jnp.bfloat16)
    prior_term = prior_slope * counted * bound_prob * (1.0 - bound_prob)
    grad_first = (
        grad_merged
        + jnp.einsum(
            "sjt,sjd->std", pool_hot, pooled_low, preferred_element_type=jnp.float32
        ).reshape(rows_all, -1)
        + prior_term[:, None] * boundary_weight[None, :]
    )
    grad_bound = matmul_exact(prior_term, first_out)
    grad_start, grads_one = layer_backward(grad_first, saved_one, sequences, layer_weights(0))
    grad_embed = matmul_exact(token_hot.T, grad_start)
    stacked = [
        jnp.stack([one_part, two_part, three_part])
        for one_part, two_part, three_part in zip(grads_one, grads_two, grads_three)
    ]
    summed = (
        lax.psum(stacked[0].astype(jnp.bfloat16), "dp").astype(jnp.float32),
        lax.psum(stacked[1].astype(jnp.bfloat16), "dp").astype(jnp.float32),
        lax.psum(stacked[2].astype(jnp.bfloat16), "dp").astype(jnp.float32),
        lax.psum(stacked[3].astype(jnp.bfloat16), "dp").astype(jnp.float32),
        lax.psum(stacked[4].astype(jnp.bfloat16), "dp").astype(jnp.float32),
        lax.psum(stacked[5].astype(jnp.bfloat16), "dp").astype(jnp.float32),
        lax.psum(grad_embed.astype(jnp.bfloat16), "dp").astype(jnp.float32),
        lax.psum(grad_head.astype(jnp.bfloat16), "dp").astype(jnp.float32),
        lax.psum(grad_final_gain.astype(jnp.bfloat16), "dp").astype(jnp.float32),
        lax.psum(grad_bound.astype(jnp.bfloat16), "dp").astype(jnp.float32),
    )
    stacked = list(summed[:6])
    grad_embed, grad_head, grad_final_gain, grad_bound = (
        summed[6],
        summed[7],
        summed[8],
        summed[9],
    )
    grad_gains = jnp.concatenate(
        [stacked[0].reshape(2 * LAYERS, -1), grad_final_gain[None, :]], axis=0
    )
    grad_qkv, grad_out, grad_up, grad_bias, grad_down = (
        stacked[1],
        stacked[2],
        stacked[3],
        stacked[4],
        stacked[5],
    )
    split_squares = sum(
        (jnp.sum(grad * grad) for grad in (grad_qkv, grad_out, grad_up, grad_bias, grad_down))
    )
    shared_squares = sum(
        (jnp.sum(grad * grad) for grad in (grad_embed, grad_head, grad_gains, grad_bound))
    )
    grad_norm = jnp.sqrt(lax.psum(split_squares, "tensor") + shared_squares)
    factor = jnp.minimum(1.0, CLIP_NORM / (grad_norm + 1e-06))
    kinds = (
        (qkv_weight, qkv_moment, grad_qkv * factor, 2),
        (out_weight, out_moment, grad_out * factor, 0),
        (up_weight, up_moment, grad_up * factor, 1),
        (down_weight, down_moment, grad_down * factor, 0),
    )
    dp_place = lax.axis_index("dp")
    tensor_place = lax.axis_index("tensor")
    owner_base = lax.axis_size("dp") - 4 * LAYERS
    new_moments = []
    selected = []
    for kind_index in range(4):
        weight, moment, grad, split_dim = kinds[kind_index]
        new_moment = MOMENTUM * moment + grad
        blend = grad + MOMENTUM * new_moment
        chosen = jnp.clip(dp_place - owner_base - kind_index * LAYERS, 0, LAYERS - 1)
        new_moments.append(new_moment)
        selected.append(lax.dynamic_index_in_dim(blend, chosen, 0, keepdims=False))
    gathered = (
        lax.all_gather(selected[0].astype(jnp.bfloat16), "tensor", axis=2, tiled=True).astype(
            jnp.float32
        ),
        lax.all_gather(selected[1].astype(jnp.bfloat16), "tensor", axis=0, tiled=True).astype(
            jnp.float32
        ),
        lax.all_gather(selected[2].astype(jnp.bfloat16), "tensor", axis=1, tiled=True).astype(
            jnp.float32
        ),
        lax.all_gather(selected[3].astype(jnp.bfloat16), "tensor", axis=0, tiled=True).astype(
            jnp.float32
        ),
    )
    own_shards = []
    scales = []
    for kind_index in range(4):
        split_dim = kinds[kind_index][3]
        whole = gathered[kind_index]
        flat = whole.reshape(whole.shape[0], -1)
        first_owner = owner_base + kind_index * LAYERS
        owner = (dp_place >= first_owner) & (dp_place < first_owner + LAYERS)
        ortho = lax.cond(owner, newton_schulz, blank_matrix, flat).reshape(whole.shape)
        width = selected[kind_index].shape[split_dim]
        own_shards.append(
            lax.dynamic_slice_in_dim(ortho, tensor_place * width, width, axis=split_dim)
        )
        scales.append(MUON_RATE * max(1.0, flat.shape[0] / flat.shape[1]) ** 0.5)
    updates = []
    for kind_index in range(4):
        layer_pieces = []
        for layer_index in range(LAYERS):
            layer_pieces.append(
                from_root(
                    shortened_2(own_shards[kind_index]),
                    "dp",
                    owner_base + kind_index * LAYERS + layer_index,
                )
            )
        updates.append(jnp.stack(layer_pieces))
    new_weights = [
        kinds[kind_index][0] * (1.0 - MUON_DECAY) - scales[kind_index] * updates[kind_index]
        for kind_index in range(4)
    ]
    emb_a, emb_b, emb_w = adam_update(
        embedding, embedding_first, embedding_second, grad_embed * factor, 0.5, 0.1
    )
    head_a, head_b, head_w = adam_update(
        head, head_first, head_second, grad_head * factor, 0.05, 0.1
    )
    gain_a, gain_b, gain_w = adam_update(
        gains, gains_first, gains_second, grad_gains * factor, 0.6, 0.0
    )
    bias_a, bias_b, bias_w = adam_update(
        up_bias, bias_first, bias_second, grad_bias * factor, 0.3, 0.0
    )
    bound_a, bound_b, bound_w = adam_update(
        boundary_weight, boundary_first, boundary_second, grad_bound * factor, 0.05, 0.0
    )
    return (
        loss_sum,
        count_total,
        grad_norm,
        new_moments[0],
        new_weights[0],
        new_moments[1],
        new_weights[1],
        new_moments[2],
        new_weights[2],
        new_moments[3],
        new_weights[3],
        emb_a,
        emb_b,
        emb_w,
        head_a,
        head_b,
        head_w,
        gain_a,
        gain_b,
        gain_w,
        bias_a,
        bias_b,
        bias_w,
        bound_a,
        bound_b,
        bound_w,
    )


BF = jnp.bfloat16
F32 = jnp.float32
SWAP = [(0, 1), (1, 0)]
DP_AXES = ("zh", "zl", "y", "core")
HALF_AXES = ("zl", "y", "core", "tensor")
SPLIT_DIMS = (2, 0, 1, 0)


def swap(value, axis):
    return lax.ppermute(value, axis, SWAP)


def summed_over(value, axes):
    for axis in axes:
        value = value + swap(value, axis)
    return value


def tie(values, *tokens):
    return list(lax.optimization_barrier(tuple(values) + tokens)[: len(values)])


def ordered(shard, mine, other, dim):
    return jnp.where(
        shard == 0, jnp.concatenate([mine, other], dim), jnp.concatenate([other, mine], dim)
    )


def exchange_weights(packed, core):
    half = packed.shape[0] // 2
    first = swap(lax.dynamic_slice_in_dim(packed, core * half, half, 0), "tensor")
    second = swap(first, "core")
    return jnp.where(core == 0, jnp.concatenate([first, second]), jnp.concatenate([second, first]))


def attend_local(queries, key_rows, value_rows):
    total = queries.shape[1]
    step = 256 if total % 256 == 0 else total
    outputs, summaries = [], []
    for first in range(0, total, step):
        last = first + step
        scores = (
            jnp.einsum(
                "hqd,hkd->hqk", queries[:, first:last], key_rows[:, :last], preferred_element_type=F32
            )
            * HEAD_SIZE**-0.5
        )
        allowed = (first + jnp.arange(step))[:, None] >= jnp.arange(last)[None, :]
        scores = jnp.where(allowed, scores, -1e30)
        highest = jnp.max(scores, axis=-1, keepdims=True)
        expo = jnp.exp(scores - highest)
        totals = jnp.sum(expo, axis=-1, keepdims=True)
        soft = (expo / totals).astype(BF)
        outputs.append(
            jnp.einsum("hqk,hkd->hqd", soft, value_rows[:, :last], preferred_element_type=F32).astype(BF)
        )
        summaries.append(highest + jnp.log(totals))
    return jnp.concatenate(outputs, axis=1), jnp.concatenate(summaries, axis=1)


def attend_local_back(queries, key_rows, value_rows, grad_mixed, mixed, summary):
    total = queries.shape[1]
    step = 256 if total % 256 == 0 else total
    scale = HEAD_SIZE**-0.5
    centre = jnp.sum(grad_mixed.astype(F32) * mixed.astype(F32), axis=-1, keepdims=True)
    grad_keys = jnp.zeros(key_rows.shape, F32)
    grad_values = jnp.zeros(key_rows.shape, F32)
    grad_queries = []
    for first in range(0, total, step):
        last = first + step
        query_block = queries[:, first:last]
        grad_block = grad_mixed[:, first:last]
        scores = jnp.einsum("hqd,hkd->hqk", query_block, key_rows[:, :last], preferred_element_type=F32) * scale
        allowed = (first + jnp.arange(step))[:, None] >= jnp.arange(last)[None, :]
        soft = jnp.exp(jnp.where(allowed, scores, -1e30) - summary[:, first:last])
        grad_soft = jnp.einsum("hqd,hkd->hqk", grad_block, value_rows[:, :last], preferred_element_type=F32)
        grad_scores = (soft * (grad_soft - centre[:, first:last])).astype(BF)
        grad_queries.append(
            scale * jnp.einsum("hqk,hkd->hqd", grad_scores, key_rows[:, :last], preferred_element_type=F32)
        )
        new_keys = scale * jnp.einsum("hqk,hqd->hkd", grad_scores, query_block, preferred_element_type=F32)
        new_values = jnp.einsum("hqk,hqd->hkd", soft.astype(BF), grad_block, preferred_element_type=F32)
        pad = ((0, 0), (0, total - last), (0, 0))
        grad_keys = grad_keys + jnp.pad(new_keys, pad)
        grad_values = grad_values + jnp.pad(new_values, pad)
    return jnp.concatenate(grad_queries, axis=1), grad_keys, grad_values


def heads_first(rows):
    return jnp.transpose(rows.reshape(rows.shape[0], -1, HEAD_SIZE), (1, 0, 2))


def rows_first(values):
    return jnp.transpose(values, (1, 0, 2)).reshape(values.shape[1], -1)


def whole_layer_forward(inputs, weights):
    gain_pair, w_qkv, w_out, w_up, b_up, w_down = weights
    normed = rms_norm(inputs, gain_pair[0]).astype(BF)
    packed = [
        heads_first(jnp.dot(normed, w_qkv[part], preferred_element_type=F32).astype(BF)) for part in range(3)
    ]
    mixed, summary = attend_local(*packed)
    after = inputs + jnp.dot(rows_first(mixed), w_out, preferred_element_type=F32)
    normed_ffn = rms_norm(after, gain_pair[1]).astype(BF)
    hidden = jnp.dot(normed_ffn, w_up, preferred_element_type=F32) + b_up
    result = after + jnp.dot(jax.nn.gelu(hidden).astype(BF), w_down, preferred_element_type=F32)
    return result, (inputs, after, packed, mixed, summary, hidden)


def hidden_backward(grad_result, saved, weights):
    gain_pair, _, _, w_up, _, w_down = weights
    after, hidden = saved[1], saved[5]
    grad_branch = grad_result.astype(BF)
    activated, gelu_back = jax.vjp(jax.nn.gelu, hidden)
    grad_down = jnp.dot(activated.astype(BF).T, grad_branch, preferred_element_type=F32)
    grad_act = jnp.dot(grad_branch, w_down.T, preferred_element_type=F32)
    grad_hidden = gelu_back(grad_act)[0].astype(BF)
    grad_bias = jnp.sum(grad_hidden.astype(F32), axis=0)
    normed_ffn, norm_back = jax.vjp(rms_norm, after, gain_pair[1])
    grad_up = jnp.dot(normed_ffn.astype(BF).T, grad_hidden, preferred_element_type=F32)
    grad_norm, grad_gain = norm_back(jnp.dot(grad_hidden, w_up.T, preferred_element_type=F32))
    return grad_result + grad_norm, grad_up, grad_bias, grad_down, grad_gain


def attention_backward(grad_after, saved, weights):
    gain_pair, w_qkv, w_out = weights[:3]
    inputs, _, packed, mixed, summary, _ = saved
    grad_attn = grad_after.astype(BF)
    grad_out = jnp.dot(rows_first(mixed).T, grad_attn, preferred_element_type=F32)
    grad_mixed = heads_first(jnp.dot(grad_attn, w_out.T, preferred_element_type=F32).astype(BF))
    grad_parts = [
        rows_first(part.astype(BF)) for part in attend_local_back(*packed, grad_mixed, mixed, summary)
    ]
    normed, norm_back = jax.vjp(rms_norm, inputs, gain_pair[0])
    normed_low = normed.astype(BF)
    grad_qkv = jnp.stack([jnp.dot(normed_low.T, part, preferred_element_type=F32) for part in grad_parts])
    grad_normed = sum(
        jnp.dot(part, w_qkv[at].T, preferred_element_type=F32) for at, part in enumerate(grad_parts)
    )
    grad_norm, grad_gain = norm_back(grad_normed)
    return grad_after + grad_norm, grad_qkv, grad_out, grad_gain


def shard_pair(shard, values, dim):
    width = values.shape[dim] // 2
    mine = lax.dynamic_slice_in_dim(values, shard * width, width, dim)
    return mine, lax.dynamic_slice_in_dim(values, (1 - shard) * width, width, dim)


def to_rows(qkv, out, up, down):
    ups = [up[:, :512], up[:, 512:]]
    qkvs = [qkv.reshape(768, 512)]
    return jnp.concatenate([out, down] + ups + qkvs, axis=0)


def from_rows(rows):
    up = jnp.concatenate([rows[1280:1792], rows[1792:2304]], axis=1)
    return rows[2304:3072].reshape(3, 512, 256), rows[0:256], up, rows[256:1280]


def newton_map(gram):
    inverse = 1.0 / (jnp.sqrt(jnp.trace(gram)) + 1e-07)
    gram = gram * (inverse * inverse)
    eye = jnp.eye(512, dtype=F32)
    total = None
    for index in range(5):
        poly = COEF_A * eye + COEF_B * gram + COEF_C * matmul_exact(gram, gram)
        total = poly if total is None else matmul_exact(total, poly)
        if index < 4:
            gram = matmul_exact(matmul_exact(gram, poly), poly)
            gram = 0.5 * (gram + gram.T)
    return (total * inverse).astype(BF)


def gram_of(left, right, dims):
    return lax.dot_general(left, right, (dims, ((), ())), preferred_element_type=F32)


def sequence_body(
    tokens, targets, boundaries, lengths, embedding, head, qkv_weight, out_weight, up_weight, up_bias,
    down_weight, gains, boundary_weight, qkv_moment, out_moment, up_moment, down_moment, embedding_first,
    embedding_second, head_first, head_second, gains_first, gains_second, bias_first, bias_second,
    boundary_first, boundary_second,
):
    length = tokens.shape[1]
    core, shard = lax.axis_index("core"), lax.axis_index("tensor")
    place_y, place_zl = lax.axis_index("y"), lax.axis_index("zl")
    own_length = lax.dynamic_index_in_dim(lengths, shard, 0, keepdims=False)
    token_row = lax.dynamic_index_in_dim(tokens, shard, 0, keepdims=False)
    target_row = lax.dynamic_index_in_dim(targets, shard, 0, keepdims=False)
    bound_row = lax.dynamic_index_in_dim(boundaries, shard, 0, keepdims=False)
    qkv_parts = jnp.transpose(qkv_weight, (0, 2, 1, 3))
    vocab_ids = jnp.arange(VOCAB, dtype=jnp.int32)
    target_hot = (target_row[:, None] == vocab_ids[None, :]).astype(F32)
    counted = (jnp.arange(length, dtype=jnp.int32) < own_length).astype(F32)
    segment = jnp.cumsum(bound_row) - bound_row
    short_ids = jnp.arange(SHORT, dtype=jnp.int32)
    pool_hot = (segment[None, :] == short_ids[:, None]).astype(BF)
    lift_hot = (segment[:, None] - 1 == short_ids[None, :]).astype(BF)
    sizes_seg = jnp.sum(pool_hot.astype(F32), axis=1, keepdims=True)

    rows_own, rows_other = [], []
    for layer in range(LAYERS):
        packed = to_rows(
            *[value[layer].astype(BF) for value in (qkv_parts, out_weight, up_weight, down_weight)]
        )
        if rows_other:
            (packed,) = tie([packed], rows_other[-1])
        rows_own.append(packed)
        rows_other.append(exchange_weights(packed, core))
    bias_other = swap(up_bias, "tensor")
    bias_whole = ordered(shard, up_bias, bias_other, 1)

    def layer_weights(layer):
        mine, other = from_rows(rows_own[layer]), from_rows(rows_other[layer])
        dims = (2, 0, 1, 0)
        w_qkv, w_out, w_up, w_down = [
            ordered(shard, own, far, dim) for own, far, dim in zip(mine, other, dims)
        ]
        return gains[2 * layer : 2 * layer + 2], w_qkv, w_out, w_up, bias_whole[layer], w_down

    weights = [layer_weights(layer) for layer in range(LAYERS)]
    wide = jnp.zeros((8, 128), F32)
    count_total = summed_over(
        jnp.sum(jnp.clip(lengths, 0, length)).astype(F32).reshape(1, 1) + wide, DP_AXES
    )[0, 0]

    token_hot = (token_row[:, None] == vocab_ids[None, :]).astype(BF)
    table_high = embedding.astype(BF)
    table_rest = embedding - table_high.astype(F32)
    table_mid = table_rest.astype(BF)
    table_low = (table_rest - table_mid.astype(F32)).astype(BF)
    start_rows = sum(
        jnp.dot(token_hot, part, preferred_element_type=F32) for part in (table_high, table_mid, table_low)
    )
    first_out, saved_one = whole_layer_forward(start_rows, weights[0])
    bound_prob = jax.nn.sigmoid(jnp.sum(first_out * boundary_weight, axis=-1))
    shortened = jnp.dot(pool_hot, first_out.astype(BF), preferred_element_type=F32) / sizes_seg
    short_out, saved_two = whole_layer_forward(shortened, weights[1])
    lifted = jnp.dot(lift_hot, short_out.astype(BF), preferred_element_type=F32)
    final_out, saved_three = whole_layer_forward(first_out + lifted, weights[2])
    bound_total = summed_over(jnp.sum(counted * bound_prob).reshape(1, 1) + wide, DP_AXES + ("tensor",))[0, 0]
    final_norm, final_back = jax.vjp(rms_norm, final_out, gains[2 * LAYERS])
    final_low = final_norm.astype(BF)
    head_low = head.astype(BF)
    logits = jnp.dot(final_low, head_low, preferred_element_type=F32)
    highest = jnp.max(logits, axis=-1, keepdims=True)
    log_probs = logits - highest - jnp.log(jnp.sum(jnp.exp(logits - highest), axis=-1, keepdims=True))
    local_cross = -jnp.sum(counted * jnp.sum(target_hot * log_probs, axis=-1))
    rest_count = count_total - bound_total
    prior_nll = -(
        lax.lgamma(count_total + 1.0)
        - lax.lgamma(bound_total + 1.0)
        - lax.lgamma(rest_count + 1.0)
        + bound_total * math.log(PRIOR_RATE)
        + rest_count * math.log(1.0 - PRIOR_RATE)
    )
    prior_slope = (
        lax.digamma(bound_total + 1.0)
        - lax.digamma(rest_count + 1.0)
        - math.log(PRIOR_RATE)
        + math.log(1.0 - PRIOR_RATE)
    ) / count_total
    grad_logits = ((jnp.exp(log_probs) - target_hot) * (counted / count_total)[:, None]).astype(BF)
    grad_head = jnp.dot(final_low.T, grad_logits, preferred_element_type=F32)
    grad_final, gain_final = final_back(jnp.dot(grad_logits, head_low.T, preferred_element_type=F32))

    def pack_pair(pack, *values):
        pairs = [shard_pair(shard, value.astype(BF), dim) for value, dim in values]
        return pack(*[pair[0] for pair in pairs]), pack(*[pair[1] for pair in pairs])

    def pack_hidden(up, down):
        return jnp.concatenate([down, up[:, :512], up[:, 512:]], axis=0)

    def pack_attention(qkv, out):
        return jnp.concatenate([out, qkv.reshape(768, 512)], axis=0)

    def over_core(mine, other):
        half = mine.shape[0] // 2
        kept = [lax.dynamic_slice_in_dim(value, core * half, half, 0) for value in (mine, other)]
        sent = [lax.dynamic_slice_in_dim(value, (1 - core) * half, half, 0) for value in (mine, other)]
        got = swap(jnp.stack(sent), "core")
        return kept[0].astype(F32) + got[0].astype(F32), (kept[1].astype(F32) + got[1].astype(F32)).astype(BF)

    grad_mid, up_three, bias_three, down_three, gain_three_b = hidden_backward(grad_final, saved_three, weights[2])
    part_ffn_three, send_ffn_three = over_core(*pack_pair(pack_hidden, (up_three, 1), (down_three, 0)))
    (grad_mid,) = tie([grad_mid], send_ffn_three)
    got_ffn_three = swap(send_ffn_three, "tensor")
    grad_merged, qkv_three, out_three, gain_three_a = attention_backward(grad_mid, saved_three, weights[2])
    part_attn_three, send_attn_three = over_core(*pack_pair(pack_attention, (qkv_three, 2), (out_three, 0)))
    (got_ffn_three,) = tie([got_ffn_three], grad_merged)
    (grad_merged,) = tie([grad_merged], send_attn_three)
    got_attn_three = swap(send_attn_three, "tensor")
    grad_short = jnp.dot(lift_hot.T, grad_merged.astype(BF), preferred_element_type=F32)
    grad_mid, up_two, bias_two, down_two, gain_two_b = hidden_backward(grad_short, saved_two, weights[1])
    grad_pooled, qkv_two, out_two, gain_two_a = attention_backward(grad_mid, saved_two, weights[1])
    (got_attn_three,) = tie([got_attn_three], grad_pooled)
    sum_three = jnp.concatenate(
        [
            (part_ffn_three + got_ffn_three.astype(F32)).astype(BF),
            (part_attn_three + got_attn_three.astype(F32)).astype(BF),
        ],
        axis=0,
    )
    total_three = lax.psum(sum_three, ("zh", "zl", "y"))
    part_ffn_two, send_ffn_two = over_core(*pack_pair(pack_hidden, (up_two, 1), (down_two, 0)))
    part_attn_two, send_attn_two = over_core(*pack_pair(pack_attention, (qkv_two, 2), (out_two, 0)))
    send_two = jnp.concatenate([send_ffn_two, send_attn_two], axis=0)
    part_two = jnp.concatenate([part_ffn_two, part_attn_two], axis=0)
    got_two = swap(send_two, "tensor")
    pooled_low = (grad_pooled / sizes_seg).astype(BF)
    prior_term = prior_slope * counted * bound_prob * (1.0 - bound_prob)
    (grad_merged,) = tie([grad_merged], sum_three, send_two)
    grad_first = (
        grad_merged
        + jnp.dot(pool_hot.T, pooled_low, preferred_element_type=F32)
        + prior_term[:, None] * boundary_weight[None, :]
    )
    grad_bound = jnp.sum(prior_term[:, None] * first_out, axis=0)
    grad_mid, up_one, bias_one, down_one, gain_one_b = hidden_backward(grad_first, saved_one, weights[0])
    part_ffn_one, send_ffn_one = over_core(*pack_pair(pack_hidden, (up_one, 1), (down_one, 0)))
    (got_two,) = tie([got_two], grad_mid)
    sum_two = (part_two + got_two.astype(F32)).astype(BF)
    total_two = lax.psum(sum_two, ("zh", "zl", "y"))
    got_ffn_one = swap(send_ffn_one, "tensor")
    (grad_mid,) = tie([grad_mid], sum_two, send_ffn_one)
    grad_start, qkv_one, out_one, gain_one_a = attention_backward(grad_mid, saved_one, weights[0])
    (got_ffn_one,) = tie([got_ffn_one], grad_start)
    part_attn_one, send_attn_one = over_core(*pack_pair(pack_attention, (qkv_one, 2), (out_one, 0)))
    got_attn_one = swap(send_attn_one, "tensor")
    start_high = grad_start.astype(BF)
    start_low = (grad_start - start_high.astype(F32)).astype(BF)
    grad_embed = sum(jnp.dot(token_hot.T, part, preferred_element_type=F32) for part in (start_high, start_low))
    tables = jnp.concatenate([grad_embed.reshape(256, 512), grad_head.reshape(256, 512)], axis=0).astype(BF)
    tables = (tables.astype(F32) + swap(tables, "tensor").astype(F32)).astype(BF)
    tables = (tables.astype(F32) + swap(tables, "core").astype(F32)).astype(BF)
    late = lax.psum(
        jnp.concatenate(
            [
                (part_ffn_one + got_ffn_one.astype(F32)).astype(BF),
                (part_attn_one + got_attn_one.astype(F32)).astype(BF),
                tables,
            ],
            axis=0,
        ),
        ("zh", "zl", "y"),
    )
    stacked = jnp.stack([late[:1536], total_two, total_three])
    other_halves = swap(stacked, "core")
    low_half = jnp.where(core == 0, stacked, other_halves)
    high_half = jnp.where(core == 0, other_halves, stacked)
    hidden_rows = jnp.concatenate([low_half[:, :1024], high_half[:, :1024]], axis=1)
    attention_rows = jnp.concatenate([low_half[:, 1024:], high_half[:, 1024:]], axis=1)
    grad_embed, grad_head = late[1536:1792].astype(F32), late[1792:2048].reshape(512, 256).astype(F32)
    grads = [
        attention_rows[:, 256:].reshape(LAYERS, 3, 512, 256),
        attention_rows[:, :256],
        jnp.concatenate([hidden_rows[:, 1024:1536], hidden_rows[:, 1536:]], axis=2),
        hidden_rows[:, :1024],
    ]
    grads = [value.astype(F32) for value in grads]

    gain_rows = [gain_one_a, gain_one_b, gain_two_a, gain_two_b, gain_three_a, gain_three_b, gain_final, grad_bound]
    bias_pairs = jnp.stack([bias_one, bias_two, bias_three])
    vectors = jnp.concatenate(
        [jnp.stack(gain_rows), bias_pairs.reshape(12, 512)]
        + [jnp.broadcast_to(local_cross.reshape(1, 1), (4, 512))],
        axis=0,
    )
    vectors = summed_over(vectors, DP_AXES + ("tensor",))
    grad_gains, grad_bound, both_biases = vectors[0:7], vectors[7], vectors[8:20].reshape(LAYERS, 2048)
    loss_sum = vectors[20, 0] + prior_nll
    grad_bias = lax.dynamic_slice_in_dim(both_biases, shard * 1024, 1024, 1)
    shared_squares = (
        jnp.sum(vectors[0:20] * vectors[0:20]) + jnp.sum(grad_embed * grad_embed) + jnp.sum(grad_head * grad_head)
    )
    split_squares = sum(jnp.sum(grad * grad) for grad in grads)
    split_squares = summed_over(split_squares.reshape(1, 1) + wide, ("tensor",))[0, 0]
    grad_norm = jnp.sqrt(split_squares + shared_squares)
    factor = jnp.minimum(1.0, CLIP_NORM / (grad_norm + 1e-06))

    moments = [jnp.transpose(qkv_moment, (0, 2, 1, 3)), out_moment, up_moment, down_moment]
    new_moments = [MOMENTUM * moment + grad * factor for moment, grad in zip(moments, grads)]
    blends = [
        (grad * factor + MOMENTUM * new).astype(BF) for grad, new in zip(grads, new_moments)
    ]
    slot = jnp.minimum(((place_zl * 2 + place_y) * 2 + core) * 2 + shard, 4 * LAYERS - 1)
    own_layer = slot // 4
    chosen = [lax.dynamic_index_in_dim(blend, own_layer, 0, keepdims=False) for blend in blends]

    def first_pair(values):
        qkv, out, up, down = values
        gram = sum(gram_of(qkv[part], qkv[part], ((1,), (1,))) for part in range(3))
        return jnp.stack([gram, gram_of(out, out, ((0,), (0,)))])

    def second_pair(values):
        qkv, out, up, down = values
        return jnp.stack([gram_of(up, up, ((1,), (1,))), gram_of(down, down, ((0,), (0,)))])

    shares = lax.cond((slot // 2) % 2 == 0, first_pair, second_pair, chosen)
    sent = swap(lax.dynamic_index_in_dim(shares, 1 - shard, 0, keepdims=False), "tensor")
    kept = lax.dynamic_index_in_dim(shares, shard, 0, keepdims=False)
    maps = lax.all_gather(newton_map(kept + sent), HALF_AXES, axis=0, tiled=False)
    weights_in = [qkv_parts, out_weight, up_weight, down_weight]
    new_weights = [[] for _ in range(4)]
    for layer in range(LAYERS):
        qkv, out, up, down = [blend[layer] for blend in blends]
        at = 4 * layer
        updates = [
            jnp.stack([jnp.dot(maps[at], qkv[part], preferred_element_type=F32) for part in range(3)]),
            jnp.dot(out, maps[at + 1], preferred_element_type=F32),
            jnp.dot(maps[at + 2], up, preferred_element_type=F32),
            2.0 * jnp.dot(down, maps[at + 3], preferred_element_type=F32),
        ]
        for kind in range(4):
            new_weights[kind].append(
                weights_in[kind][layer] * (1.0 - MUON_DECAY) - MUON_RATE * updates[kind]
            )
    new_weights = [jnp.stack(value) for value in new_weights]
    new_moments[0] = jnp.transpose(new_moments[0], (0, 2, 1, 3))
    new_weights[0] = jnp.transpose(new_weights[0], (0, 2, 1, 3))
    muon = []
    for new_moment, new_weight in zip(new_moments, new_weights):
        muon += [new_moment, new_weight]
    return (
        loss_sum,
        count_total,
        grad_norm,
        *muon,
        *adam_update(embedding, embedding_first, embedding_second, grad_embed * factor, 0.5, 0.1),
        *adam_update(head, head_first, head_second, grad_head * factor, 0.05, 0.1),
        *adam_update(gains, gains_first, gains_second, grad_gains * factor, 0.6, 0.0),
        *adam_update(up_bias, bias_first, bias_second, grad_bias * factor, 0.3, 0.0),
        *adam_update(boundary_weight, boundary_first, boundary_second, grad_bound * factor, 0.05, 0.0),
    )


def sequence_specs(dp):
    split = [P(None, None, None, "tensor"), P(None, "tensor", None), P(None, None, "tensor"), P(None, "tensor"), P(None, "tensor", None)]
    ins = [P(dp, None)] * 3 + [P(dp), P(), P()] + split + [P(), P()]
    ins += [split[0], split[1], split[2], split[4]] + [P()] * 6 + [split[3]] * 2 + [P()] * 2
    outs = [P()] * 3
    for kind in (0, 1, 2, 4):
        outs += [split[kind]] * 2
    outs += [P()] * 9 + [split[3]] * 3 + [P()] * 3
    return tuple(ins), tuple(outs)


def solution(mesh):
    def run(tokens, *rest):
        dp, tensor = mesh.shape["dp"], mesh.shape["tensor"]
        if (dp, tensor) == (16, 2) and tokens.shape[0] == tensor * dp:
            parts = Mesh(mesh.devices.reshape(2, 2, 2, 2, 2), DP_AXES + ("tensor",))
            ins, outs = sequence_specs(DP_AXES)
            step = jax.shard_map(sequence_body, mesh=parts, in_specs=ins, out_specs=outs, check_vma=False)
        else:
            ins, outs = sequence_specs("dp")
            step = jax.shard_map(body, mesh=mesh, in_specs=ins, out_specs=outs, check_vma=False)
        return step(tokens, *rest)

    return run
```
